32 devices in a mesh: ens: 2 (over y), region: 4 (over z), bin: 2 (over x), pt: 2 (over core).
Axes of the slice: x: 2, y: 2, z: 4, core: 2. Of those that a mesh axis runs over, the one named last changes fastest.
Arguments:
- spectrum: float32 [864, 64, 512], P('ens', ('region', 'bin'), 'pt'), parts along dimension 0, may hold values from 0.1 to 2
- wind_u: float32 [128, 512], P(('ens', 'region', 'bin'), 'pt'), parts along dimension 0, may hold values from -5 to 5
- wind_v: float32 [128, 512], P(('ens', 'region', 'bin'), 'pt'), parts along dimension 0, may hold values from -5 to 5
- sea_mask: int32 [64, 512], P('region', 'pt'), may hold values from 0 to 1, as said below
- depth_factor: float32 [64, 512], P('region', 'pt'), may hold values from 0.4 to 1
- slope_x: float32 [64, 512], P('region', 'pt'), may hold values from -0.5 to 0.5
- slope_y: float32 [64, 512], P('region', 'pt'), may hold values from -0.5 to 0.5
Outputs:
- updated: float32 [864, 64, 512], P('ens', ('region', 'bin'), 'pt'), parts along dimension 0
The draws below stay inside these ranges and needn't reach their ends.
There are 2 independent parts, one for each index of `ens`. The reference program is written for one: setup_inputs(seed, part) draws one part's arguments, and reference() takes and returns one part's arrays. A program takes and returns all parts, laid end to end along the dimension named above; an argument that names none is the same for every part. Nothing has to cross between parts.
Inputs may be any that keep to these rules, and one draw needn't show every extreme that they name: `sea_mask`: the grid's first and last rows are land.
All inputs are finite; a program needn't handle non-finite values.
Results may differ from the reference program's by a relative error of at most 0.00002.
Values sent between devices are 32-bit elements; how exact they have to be, the bound alone decides.
No kernel may reach another device: no remote copies, remote signals or barrier semaphores. Data moves between devices by JAX's collectives and lax.ppermute only.
A program may use at most 128 MiB of HBM per device.

```python
import math
import jax
import jax.numpy as jnp
from jax import lax

F = 12
DIRS = 36
SUB = 4
K = 432
NY = 64
NX = 512


def draw_sea_mask(key, part):
    key = jax.random.fold_in(key, 7)
    rows = jnp.arange(NY, dtype=jnp.int32)[:, None]
    limit = 150 + 450 * rows // NY
    rolls = jax.random.randint(key, (NY, NX), 0, 1000)
    inside = (rows > 0) & (rows < NY - 1)
    return jnp.where((rolls >= limit) & inside, 1, 0).astype(jnp.int32)


def shard_levels(key, shape, cuts, low, top_value):
    gain, own = 1.0, jax.random.fold_in(key, 6)
    for dim, blocks in cuts:
        heights = jnp.exp(jax.random.uniform(jax.random.fold_in(own, dim), (blocks,), jnp.float32, low / len(cuts), top_value / len(cuts)))
        gain = gain * jnp.repeat(heights, shape[dim] // blocks).reshape([-1 if axis == dim else 1 for axis in range(len(shape))])
    return gain


def gaussian(stream_key, shape, deviation, reach, shards=(), kind=jnp.bfloat16):
    values = jax.random.normal(stream_key, shape, jnp.float32) * deviation
    if len(shards) > 0:
        values = shard_levels(stream_key, shape, shards, -0.22, 0.18) * values
    return jnp.clip(values, min=-reach, max=reach).astype(kind)


def setup_inputs(seed: int = 0, part: int = 0) -> dict:
    key_list = jax.random.split(jax.random.key(seed), 8)
    part_splits = jax.random.split(jax.random.fold_in(key_list[7], part), 8)
    spectrum = jnp.clip(jnp.exp(math.log(2.0) - 2.9957323 * jax.random.uniform(part_splits[0], (K, NY, NX), jnp.float32) ** shard_levels(part_splits[0], (K, NY, NX), ((1, 8), (2, 2)), -0.2, 0.2)), 0.1, 2.0)
    wind_u = gaussian(part_splits[1], (NY, NX), 1.0, 5.0, ((0, 8), (1, 2)), jnp.float32)
    wind_v = gaussian(part_splits[2], (NY, NX), 1.0, 5.0, ((0, 8), (1, 2)), jnp.float32)
    sea_mask = draw_sea_mask(jax.random.fold_in(key_list[7], 71), part)
    depth_factor = jnp.clip(0.4 + 0.6 * jax.random.uniform(key_list[4], (NY, NX), jnp.float32) ** shard_levels(key_list[4], (NY, NX), ((0, 4), (1, 2)), -0.2, 0.2), 0.4, 1.0)
    slope_x = jnp.clip(jax.random.uniform(key_list[5], (NY, NX), jnp.float32, -0.5, 0.5) * shard_levels(key_list[5], (NY, NX), ((0, 4), (1, 2)), -0.4, 0.0), -0.5, 0.5)
    slope_y = jnp.clip(jax.random.uniform(key_list[6], (NY, NX), jnp.float32, -0.5, 0.5) * shard_levels(key_list[6], (NY, NX), ((0, 4), (1, 2)), -0.4, 0.0), -0.5, 0.5)
    return {"spectrum": spectrum, "wind_u": wind_u, "wind_v": wind_v, "sea_mask": sea_mask, "depth_factor": depth_factor, "slope_x": slope_x, "slope_y": slope_y}


def update(field, west, east, south, north, speed, turn, cos_t, sin_t, depth, slope_x, slope_y, maskf):
    vx = speed * depth * cos_t
    vy = speed * depth * sin_t
    vt = turn * (sin_t * slope_x - cos_t * slope_y)
    before = jnp.roll(field, 1, axis=-3)
    after = jnp.roll(field, -1, axis=-3)
    change = jnp.maximum(vx, 0.0) * (field - west) + jnp.minimum(vx, 0.0) * (east - field)
    change = change + jnp.maximum(vy, 0.0) * (field - south) + jnp.minimum(vy, 0.0) * (north - field)
    change = change + jnp.maximum(vt, 0.0) * (field - before) + jnp.minimum(vt, 0.0) * (after - field)
    return (field - change) * maskf


def reference(spectrum, wind_u, wind_v, sea_mask, depth_factor, slope_x, slope_y):
    sigma = 0.6 * 1.1 ** jnp.arange(F, dtype=jnp.float32)
    weight = sigma / (DIRS * jnp.sum(sigma))
    angles = 2.0 * jnp.pi * jnp.arange(DIRS, dtype=jnp.float32) / DIRS
    cos_t = jnp.cos(angles)[:, None, None]
    sin_t = jnp.sin(angles)[:, None, None]
    maskf = sea_mask.astype(jnp.float32)
    spec4 = spectrum.reshape(F, DIRS, NY, NX)
    per_freq = jnp.sum(spec4, axis=1)
    energy = jnp.sum(weight[:, None, None] * per_freq, axis=0)
    first = jnp.sum((weight * sigma)[:, None, None] * per_freq, axis=0)
    mean_sigma = first / energy
    steep = energy * mean_sigma * mean_sigma / 1.5
    lean = wind_u * cos_t + wind_v * sin_t

    def one_freq(item):
        field, sig = item
        speed = 0.27 / sig
        turn = 0.5 * speed
        push = jnp.maximum(lean, 0.0)
        growth = 0.5 * sig * push * push
        damping = 0.5 * (sig / mean_sigma) * steep * steep
        field = field * (1.0 + growth) / (1.0 + damping) * maskf
        for step in range(SUB):
            west = jnp.roll(field, 1, axis=2)
            east = jnp.roll(field, -1, axis=2)
            south = jnp.roll(field, 1, axis=1)
            north = jnp.roll(field, -1, axis=1)
            field = update(field, west, east, south, north, speed, turn, cos_t, sin_t, depth_factor, slope_x, slope_y, maskf)
        return field

    result = lax.map(one_freq, (spec4, sigma))
    return result.reshape(K, NY, NX)
```

```python
import math

import jax
import jax.numpy as jnp
import numpy as np
from jax import lax
from jax.experimental import pallas as pl
from jax.experimental.pallas import tpu as pltpu
from jax.sharding import PartitionSpec as P

F = 12
DIRS = 36
SUB = 4
ROWS = 8
LANES = 128
TILES = 2
RING = TILES + 1
HALF = DIRS // 2
SENT = [HALF - 1 + 2 * (SUB - k) for k in range(1, SUB + 1)]
PACK = sum(SENT)
GEO = 16
CHUNKS = (5, 5, 2)
PER = 12

SIGMA = 0.6 * 1.1 ** np.arange(F, dtype=np.float64)
WEIGHT = SIGMA / (DIRS * SIGMA.sum())


def quarter_exact(fn):
    values = np.array([fn(2.0 * math.pi * d / DIRS) for d in range(DIRS)])
    values[np.abs(values) < 1e-9] = 0.0
    return values


COS = quarter_exact(math.cos)
SIN = quarter_exact(math.sin)
TABLE = np.zeros((6, 64), np.float32)
TABLE[0, :DIRS] = COS
TABLE[1, :DIRS] = SIN
TABLE[2, :F] = SIGMA
TABLE[3, :F] = WEIGHT
TABLE[4, :F] = WEIGHT * SIGMA
TABLE[5, :F] = 0.27 / SIGMA


def segments(up):
    out, row = [], 0
    for k in range(1, SUB + 1):
        low = 1 - (SUB - k) + (0 if up else HALF)
        left, at = SENT[k - 1], low
        while left > 0:
            first = at % DIRS
            count = min(left, DIRS - first)
            out.append((k, first, count, row))
            row, at, left = row + count, at + count, left - count
    return out


def lane_iota(shape):
    return lax.broadcasted_iota(jnp.int32, shape, len(shape) - 1)


def edge_columns(first_tile, last_tile):
    return jnp.where(lane_iota(first_tile.shape) < LANES // 2, first_tile, last_tile)


def put_edges(packed, value, slot):
    lanes = lane_iota(packed.shape)
    rolled = pltpu.roll(value, SUB + 8 * slot, 1)
    return jnp.where((lanes >= 8 * slot) & (lanes < 8 * slot + 8), rolled, packed)


def get_edges(packed, slot):
    return pltpu.roll(packed, LANES - SUB - 8 * slot if isinstance(slot, int) else lax.rem(2 * LANES - SUB - 8 * slot, LANES), 1)


def source_kernel(
    spec_hbm, u_ref, v_ref, mask_ref, depth_ref, sx_ref, sy_ref, tab,
    src_hbm, geo_own, *rest,
):
    n = len(CHUNKS)
    ups, downs = rest[:n], rest[n : 2 * n]
    edge_ref, corner_up, corner_down, raw, src, push, line, in_sem, out_sem = rest[2 * n :]

    def load(f, t):
        return pltpu.make_async_copy(
            spec_hbm.at[pl.ds(f * DIRS, DIRS), :, pl.ds(t * LANES, LANES)],
            raw.at[t, pl.ds(f * DIRS, DIRS)],
            in_sem.at[f, t],
        )

    def store(f):
        rows = pl.ds(f * DIRS * ROWS, DIRS * ROWS)
        return pltpu.make_async_copy(src.at[:, rows], src_hbm.at[:, rows], out_sem.at[f])

    for f in range(F):
        for t in range(TILES):
            load(f, t).start()

    off = pl.multiple_of(lax.axis_index("bin") * ROWS, ROWS)
    own = pl.ds(off, ROWS)
    mask = mask_ref[own, :].astype(jnp.float32)
    geo = (depth_ref[own, :] * mask, sx_ref[own, :] * mask, sy_ref[own, :] * mask)
    for g in range(3):
        geo_own[g * ROWS : (g + 1) * ROWS, :] = geo[g]
        rows = CHUNKS[0] * PACK + g * SUB
        ups[0][rows : rows + SUB, :] = geo[g][ROWS - SUB :, :]
        downs[0][rows : rows + SUB, :] = geo[g][:SUB, :]
    tail = CHUNKS[0] * PACK + 3 * SUB
    ups[0][tail : tail + GEO - 3 * SUB, :] = jnp.zeros((GEO - 3 * SUB, TILES * LANES), jnp.float32)
    downs[0][tail : tail + GEO - 3 * SUB, :] = jnp.zeros((GEO - 3 * SUB, TILES * LANES), jnp.float32)

    u, v = u_ref[...], v_ref[...]

    def push_body(d, c):
        lean = jnp.maximum(u * tab[0, d] + v * tab[1, d], 0.0)
        half = 0.5 * lean * lean
        for t in range(TILES):
            push[t, d] = half[:, t * LANES : (t + 1) * LANES]
        return c

    lax.fori_loop(0, DIRS, push_body, 0)

    def energy_body(f, carry):
        energy, first = carry
        for t in range(TILES):
            load(f, t).wait()
        sums = []
        for t in range(TILES):
            parts = [raw[t, f * DIRS + d] for d in range(4)]
            for d in range(4, DIRS):
                parts[d % 4] = parts[d % 4] + raw[t, f * DIRS + d]
            sums.append((parts[0] + parts[1]) + (parts[2] + parts[3]))
        total = jnp.concatenate(sums, axis=1)
        return energy + tab[3, f] * total, first + tab[4, f] * total

    zero = jnp.zeros((ROWS, TILES * LANES), jnp.float32)
    energy, first = lax.fori_loop(0, F, energy_body, (zero, zero))
    mean_sigma = first / energy
    steep = energy * mean_sigma * mean_sigma / 1.5
    damp = 0.5 * steep * steep / mean_sigma

    def freq(f, local, up_ref, down_ref):
        inverse = mask / (1.0 + tab[2, f] * damp)
        sig = tab[2, f]

        def dir_body(d, c):
            for t in range(TILES):
                grown = raw[t, f * DIRS + d] * (1.0 + sig * push[t, d])
                row = pl.multiple_of((f * DIRS + d) * ROWS, ROWS)
                src[t, pl.ds(row, ROWS), :] = grown * inverse[:, t * LANES : (t + 1) * LANES]
            return c

        lax.fori_loop(0, DIRS, dir_body, 0, unroll=4)
        store(f).start()
        base = f * DIRS * ROWS
        for ref, up, corner in ((up_ref, True, corner_up), (down_ref, False, corner_down)):
            for k, d0, count, row in segments(up):
                j = ROWS - k if up else k - 1
                for t in range(TILES):
                    line[row : row + count, t * LANES : (t + 1) * LANES] = src[
                        t, pl.ds(base + d0 * ROWS + j, count, stride=ROWS), :
                    ]
            packed = jnp.zeros((ROWS, LANES), jnp.float32)
            for m in range(PACK // ROWS):
                part = line[m * ROWS : (m + 1) * ROWS, :]
                ref[pl.ds(pl.multiple_of(local * PACK + m * ROWS, ROWS), ROWS), :] = part
                packed = put_edges(packed, edge_columns(part[:, :LANES], part[:, LANES:]), m)
            corner[f] = packed
        for q in range(DIRS // PER):
            packed = jnp.zeros((ROWS, LANES), jnp.float32)
            for m in range(PER):
                rows = pl.ds(pl.multiple_of(base + (q * PER + m) * ROWS, ROWS), ROWS)
                packed = put_edges(packed, edge_columns(src[0, rows, :], src[1, rows, :]), m)
            edge_ref[f * (DIRS // PER) + q] = packed

    at = 0
    for c, count in enumerate(CHUNKS):
        def body(local, carry, c=c, at=at):
            freq(at + local, local, ups[c], downs[c])
            return carry

        lax.fori_loop(0, count, body, 0)
        at += count

    packed = jnp.zeros((ROWS, LANES), jnp.float32)
    for g in range(3):
        packed = put_edges(packed, edge_columns(geo[g][:, :LANES], geo[g][:, LANES:]), g)
    edge_ref[F * (DIRS // PER)] = packed
    for ref, corner in ((ups[0], corner_up), (downs[0], corner_down)):
        packed = jnp.zeros((ROWS, LANES), jnp.float32)
        for m in range(GEO // ROWS):
            rows = slice(CHUNKS[0] * PACK + m * ROWS, CHUNKS[0] * PACK + (m + 1) * ROWS)
            packed = put_edges(packed, edge_columns(ref[rows, :LANES], ref[rows, LANES:]), m)
        corner[F] = packed
    for f in range(F):
        store(f).wait()


def wrap(d):
    return jnp.where(d < 0, d + DIRS, jnp.where(d >= DIRS, d - DIRS, d))


def step_kernel(first, start, *refs):
    if first:
        (tab, src, up, down, edge, corner_up, corner_down,
         geo_own, geo_up, geo_down, edge_geo, corner_up_geo, corner_down_geo,
         out, geo, field_a, field_b, turn) = refs
    else:
        (tab, src, up, down, edge, corner_up, corner_down, geo, _, out, field_a, field_b, turn) = refs
    width = RING * LANES

    @pl.when(pl.program_id(0) == 0)
    def _():
        if first:
            cu = jnp.concatenate([get_edges(corner_up_geo[0], m) for m in range(2)], axis=0)
            cd = jnp.concatenate([get_edges(corner_down_geo[0], m) for m in range(2)], axis=0)
            for g in range(3):
                rows = slice(g * SUB, (g + 1) * SUB)
                own = jnp.concatenate(
                    [geo_own[g * ROWS : (g + 1) * ROWS, :], get_edges(edge_geo[0], g)], axis=1
                )
                north = jnp.concatenate([geo_down[rows, :], cd[rows, :]], axis=1)
                south = jnp.concatenate([geo_up[rows, :], cu[rows, :]], axis=1)
                geo[g] = jnp.concatenate([own, north, south], axis=0)
        zero = jnp.zeros((RING, DIRS * 2 * ROWS, LANES), jnp.float32)
        field_a[...] = zero
        sx, sy = geo[1], geo[2]

        def turn_body(d, c):
            turn[d] = 0.5 * (tab[1, d] * sx - tab[0, d] * sy)
            return c

        lax.fori_loop(0, DIRS, turn_body, 0)

    def own_body(d, c):
        row = pl.multiple_of(d * 2 * ROWS, ROWS)
        for t in range(TILES):
            field_a[t, pl.ds(row, ROWS), :] = src[t, pl.ds(pl.multiple_of(d * ROWS, ROWS), ROWS), :]
        return c

    lax.fori_loop(0, DIRS, own_body, 0, unroll=4)
    for q in range(DIRS // PER):
        packed = edge[q]
        for m in range(PER):
            row = (q * PER + m) * 2 * ROWS
            field_a[TILES, row : row + ROWS, :] = get_edges(packed, m)
    for ref, is_up, corner in ((up, True, corner_up), (down, False, corner_down)):
        packed = corner[0]
        columns = jnp.concatenate([get_edges(packed, m) for m in range(PACK // ROWS)], axis=0)
        for k, d0, count, row in segments(is_up):
            j = ROWS + (ROWS - k if is_up else k - 1)
            place = pl.ds(d0 * 2 * ROWS + j, count, stride=2 * ROWS)
            for t in range(TILES):
                field_a[t, place, :] = ref[row : row + count, t * LANES : (t + 1) * LANES]
            field_a[TILES, place, :] = columns[row : row + count, :]

    speed = tab[5, start + pl.program_id(0)]

    def load(ref, d, rows, tiles):
        row = pl.multiple_of(d * 2 * ROWS, ROWS)
        return jnp.concatenate([ref[t, pl.ds(row, rows), :] for t in range(tiles)], axis=1)

    def advance(old, new, last):
        rows, tiles = (ROWS, TILES) if last else (2 * ROWS, RING)
        depth = geo[0][:rows, : tiles * LANES]
        for quarter in range(4):
            west, south = quarter in (0, 3), quarter in (0, 1)

            def body(i, c):
                d = quarter * (DIRS // 4) + i
                whole = load(old, d, 2 * ROWS, RING)
                up_x = pltpu.roll(whole, 1 if west else width - 1, 1)[:rows, : tiles * LANES]
                up_y = pltpu.roll(whole, 1 if south else 2 * ROWS - 1, 0)[:rows, : tiles * LANES]
                now = whole[:rows, : tiles * LANES]
                before = load(old, wrap(d - 1), rows, tiles)
                after = load(old, wrap(d + 1), rows, tiles)
                vt = turn[d][:rows, : tiles * LANES]
                up_t = jnp.where(vt > 0.0, before, after)
                cos, sin = jnp.abs(tab[0, d]), jnp.abs(tab[1, d])
                moved = depth * (cos * (now - up_x) + sin * (now - up_y)) + jnp.abs(vt) * (now - up_t)
                value = now - speed * moved
                if last:
                    out[d] = value
                else:
                    row = pl.multiple_of(d * 2 * ROWS, ROWS)
                    for t in range(tiles):
                        new[t, pl.ds(row, rows), :] = value[:, t * LANES : (t + 1) * LANES]
                return c

            lax.fori_loop(0, DIRS // 4, body, 0, unroll=3)

    fields = (field_a, field_b)
    for step in range(SUB):
        advance(fields[step % 2], fields[(step + 1) % 2], step == SUB - 1)


def per_device(spectrum, wind_u, wind_v, sea_mask, depth_factor, slope_x, slope_y):
    nbins, rows, cols = spectrum.shape
    assert (nbins, rows, cols) == (F * DIRS, ROWS, TILES * LANES)
    f32 = jnp.float32
    shape = jax.ShapeDtypeStruct
    tab = jnp.asarray(TABLE)
    smem, vmem, hbm = (
        pl.BlockSpec(memory_space=pltpu.SMEM),
        pl.BlockSpec(memory_space=pltpu.VMEM),
        pl.BlockSpec(memory_space=pl.ANY),
    )
    n = len(CHUNKS)
    heights = [c * PACK + (GEO if i == 0 else 0) for i, c in enumerate(CHUNKS)]
    packs = [shape((h, cols), f32) for h in heights]
    groups = DIRS // PER
    outs = pl.pallas_call(
        source_kernel,
        out_shape=[
            shape((TILES, nbins * rows, LANES), f32),
            shape((3 * rows, cols), f32),
            *packs,
            *packs,
            shape((F * groups + 1, rows, LANES), f32),
            shape((F + 1, rows, LANES), f32),
            shape((F + 1, rows, LANES), f32),
        ],
        in_specs=[hbm] + [vmem] * 6 + [smem],
        out_specs=[hbm] + [vmem] * (2 * n + 4),
        scratch_shapes=[
            pltpu.VMEM((TILES, nbins, rows, LANES), f32),
            pltpu.VMEM((TILES, nbins * rows, LANES), f32),
            pltpu.VMEM((TILES, DIRS, rows, LANES), f32),
            pltpu.VMEM((PACK, cols), f32),
            pltpu.SemaphoreType.DMA((F, TILES)),
            pltpu.SemaphoreType.DMA((F,)),
        ],
        compiler_params=pltpu.CompilerParams(vmem_limit_bytes=32 * 2**20),
        cost_estimate=pl.CostEstimate(flops=20_000_000, bytes_accessed=9_000_000, transcendentals=0),
        name="source",
    )(spectrum, wind_u, wind_v, sea_mask, depth_factor, slope_x, slope_y, tab)
    src, geo_own = outs[:2]
    ups, downs = outs[2 : 2 + n], outs[2 + n : 2 + 2 * n]
    edge, corner_up, corner_down = outs[2 + 2 * n :]

    blocks = lax.axis_size("region") * lax.axis_size("bin")
    up_pairs = [(i, i + 1) for i in range(blocks - 1)]
    down_pairs = [(j, i) for i, j in up_pairs]
    line = ("region", "bin")

    def crossed(pairs):
        return [(2 * i + p, 2 * j + 1 - p) for i, j in pairs for p in range(2)]

    assert lax.axis_size("pt") == 2
    edge = lax.ppermute(edge, "pt", [(0, 1), (1, 0)])
    corner_up = lax.ppermute(corner_up, line + ("pt",), crossed(up_pairs))
    corner_down = lax.ppermute(corner_down, line + ("pt",), crossed(down_pairs))
    from_south = [lax.ppermute(x, line, up_pairs) for x in ups]
    from_north = [lax.ppermute(x, line, down_pairs) for x in downs]

    block = lambda s, index: pl.BlockSpec(s, index)
    width = RING * LANES
    start, geo, result = 0, None, None
    for c, count in enumerate(CHUNKS):
        first = c == 0
        at = start
        operands = [tab, src, from_south[c], from_north[c], edge, corner_up, corner_down]
        in_specs = [
            smem,
            block((TILES, DIRS * rows, LANES), lambda i, at=at: (0, at + i, 0)),
            block((PACK, cols), lambda i: (i, 0)),
            block((PACK, cols), lambda i: (i, 0)),
            block((groups, rows, LANES), lambda i, at=at: (at + i, 0, 0)),
            block((1, rows, LANES), lambda i, at=at: (at + i, 0, 0)),
            block((1, rows, LANES), lambda i, at=at: (at + i, 0, 0)),
        ]
        out_shape = [shape((nbins, rows, cols), f32)]
        out_specs = [block((DIRS, rows, cols), lambda i, at=at: (at + i, 0, 0))]
        aliases = {}
        if first:
            geo_row = count * PACK // GEO
            operands += [geo_own, from_south[c], from_north[c], edge, corner_up, corner_down]
            in_specs += [
                block((3 * rows, cols), lambda i: (0, 0)),
                block((GEO, cols), lambda i, g=geo_row: (g, 0)),
                block((GEO, cols), lambda i, g=geo_row: (g, 0)),
                block((1, rows, LANES), lambda i: (F * groups, 0, 0)),
                block((1, rows, LANES), lambda i: (F, 0, 0)),
                block((1, rows, LANES), lambda i: (F, 0, 0)),
            ]
            out_shape.append(shape((3, 2 * rows, width), f32))
            out_specs.append(block((3, 2 * rows, width), lambda i: (0, 0, 0)))
        else:
            operands += [geo, result]
            in_specs += [block((3, 2 * rows, width), lambda i: (0, 0, 0)), hbm]
            aliases = {len(operands) - 1: 0}

        def kernel(*refs, first=first, at=at):
            step_kernel(first, at, *refs)

        outs = pl.pallas_call(
            kernel,
            grid=(count,),
            out_shape=out_shape,
            in_specs=in_specs,
            out_specs=out_specs,
            scratch_shapes=[
                pltpu.VMEM((RING, DIRS * 2 * rows, LANES), f32),
                pltpu.VMEM((RING, DIRS * 2 * rows, LANES), f32),
                pltpu.VMEM((DIRS, 2 * rows, width), f32),
            ],
            input_output_aliases=aliases,
            compiler_params=pltpu.CompilerParams(vmem_limit_bytes=32 * 2**20),
            cost_estimate=pl.CostEstimate(
                flops=count * 9_000_000, bytes_accessed=count * 800_000, transcendentals=0
            ),
            name=f"steps_{c}",
        )(*operands)
        result = outs[0]
        if first:
            geo = outs[1]
        start += count
    return result


def solution(mesh):
    in_specs = (
        P("ens", ("region", "bin"), "pt"),
        P(("ens", "region", "bin"), "pt"),
        P(("ens", "region", "bin"), "pt"),
        P("region", "pt"),
        P("region", "pt"),
        P("region", "pt"),
        P("region", "pt"),
    )
    out_specs = P("ens", ("region", "bin"), "pt")
    return jax.shard_map(
        per_device, mesh=mesh, in_specs=in_specs, out_specs=out_specs, check_vma=False
    )
```

```python
import math

import jax
import jax.numpy as jnp
import numpy as np
from jax import lax
from jax.experimental import pallas as pl
from jax.experimental.pallas import tpu as pltpu
from jax.sharding import PartitionSpec as P

F = 12
DIRS = 36
SUB = 4
ROWS = 8
LANES = 128
TILES = 2
HALF = DIRS // 2
SENT = [HALF - 1 + 2 * (SUB - k) for k in range(1, SUB + 1)]
PACK = sum(SENT)
GEO = 16
CHUNKS = (6, 4, 2)
STRIP = 2 * SUB + 2
EDGES = DIRS + 3
EDGE_ROWS = 96
PITCH = ROWS + 2 * SUB
PAD = 8
HEIGHT = DIRS * PITCH + 2 * PAD
SPAN = DIRS * ROWS

SIGMA = 0.6 * 1.1 ** np.arange(F, dtype=np.float64)
WEIGHT = SIGMA / (DIRS * SIGMA.sum())


def quarter_exact(fn):
    values = np.array([fn(2.0 * math.pi * d / DIRS) for d in range(DIRS)])
    values[np.abs(values) < 1e-9] = 0.0
    return [float(x) for x in values]


COS = quarter_exact(math.cos)
SIN = quarter_exact(math.sin)
SPEED = 0.27 / SIGMA


def of_freq(values, f):
    if isinstance(f, int):
        return float(values[f])
    out = jnp.float32(values[0])
    for i in range(1, F):
        out = jnp.where(f == i, jnp.float32(values[i]), out)
    return out


HBM = pl.BlockSpec(memory_space=pltpu.HBM)
VMEM = pl.BlockSpec(memory_space=pltpu.VMEM)
ANY = pl.BlockSpec(memory_space=pl.ANY)


def segments(up):
    out, row = [], 0
    for k in range(1, SUB + 1):
        low = 1 - (SUB - k) + (0 if up else HALF)
        left, at = SENT[k - 1], low
        while left > 0:
            first = at % DIRS
            count = min(left, DIRS - first)
            out.append((k, first, count, row))
            row, at, left = row + count, at + count, left - count
    return out


def lane_iota():
    return lax.broadcasted_iota(jnp.int32, (ROWS, LANES), 1)


def own_lanes():
    own = jnp.zeros((ROWS, LANES), jnp.bool_)
    for f in range(F):
        own = own | (lane_iota() == f * STRIP + SUB) | (lane_iota() == f * STRIP + SUB + 1)
    return own


def put_edges(pairs):
    lanes = lane_iota()
    packed = jnp.zeros((ROWS, LANES), jnp.float32)
    for f, (first_tile, last_tile) in enumerate(pairs):
        ends = jnp.where(lanes < LANES // 2, first_tile, last_tile)
        at = f * STRIP
        packed = jnp.where(lanes >= at, pltpu.roll(ends, (at + SUB) % LANES, 1), packed)
        packed = jnp.where(lanes >= at + SUB + 1, pltpu.roll(ends, (at + SUB + 2) % LANES, 1), packed)
    return packed


def split(value):
    return value[:, :LANES], value[:, LANES:]


def make_sources(raw, src, push, inverse, f, base):
    sig = of_freq(SIGMA, f)
    for t in range(TILES):
        for d in range(DIRS):
            grown = raw[t, f * DIRS + d] * (1.0 + sig * push[t, d])
            row = base + d * ROWS
            src[t, pl.ds(row, ROWS), :] = grown * inverse[t]


def make_packs(src, base, local, line, up_ref, down_ref):
    for ref, up in ((up_ref, True), (down_ref, False)):
        for k, d0, count, row in segments(up):
            j = ROWS - k if up else k - 1
            for t in range(TILES):
                line[t, row : row + count, :] = src[t, pl.ds(base + d0 * ROWS + j, count, stride=ROWS), :]
        for m in range(PACK // ROWS):
            rows = pl.ds(pl.multiple_of(local * PACK + m * ROWS, ROWS), ROWS)
            for t in range(TILES):
                ref[rows, t * LANES : (t + 1) * LANES] = line[t, m * ROWS : (m + 1) * ROWS, :]


def head_kernel(
    spec, u_hbm, v_hbm, mask_hbm, depth_hbm, sx_hbm, sy_hbm,
    raw, src0, push, damp_ref, geo, up_ref, down_ref,
    u_ref, v_ref, mask_ref, depth_ref, sx_ref, sy_ref, line, small_sem, in_sem,
):
    off = pl.multiple_of(lax.axis_index("bin") * ROWS, ROWS)
    own = pl.ds(off, ROWS)
    small = [
        pltpu.make_async_copy(a, b, small_sem.at[i])
        for i, (a, b) in enumerate(
            (
                (u_hbm, u_ref),
                (v_hbm, v_ref),
                (mask_hbm.at[own], mask_ref),
                (depth_hbm.at[own], depth_ref),
                (sx_hbm.at[own], sx_ref),
                (sy_hbm.at[own], sy_ref),
            )
        )
    ]

    def load(f, t):
        return pltpu.make_async_copy(
            spec.at[pl.ds(f * DIRS, DIRS), :, pl.ds(t * LANES, LANES)],
            raw.at[t, pl.ds(f * DIRS, DIRS)],
            in_sem.at[f, t],
        )

    for copy in small:
        copy.start()
    for f in range(F):
        for t in range(TILES):
            load(f, t).start()
    for copy in small:
        copy.wait()

    mask = mask_ref[...].astype(jnp.float32)
    fields = (depth_ref[...] * mask, sx_ref[...] * mask, sy_ref[...] * mask)
    tail = CHUNKS[0] * PACK
    for g in range(3):
        for t, tile in enumerate(split(fields[g])):
            geo[g, t] = tile
        rows = slice(tail + g * SUB, tail + (g + 1) * SUB)
        up_ref[rows, :] = fields[g][ROWS - SUB :, :]
        down_ref[rows, :] = fields[g][:SUB, :]
    for ref in (up_ref, down_ref):
        ref[tail + 3 * SUB : tail + GEO, :] = jnp.zeros((GEO - 3 * SUB, TILES * LANES), jnp.float32)
    for t, tile in enumerate(split(mask)):
        geo[3, t] = tile
    u, v = split(u_ref[...]), split(v_ref[...])
    for d in range(DIRS):
        for t in range(TILES):
            lean = jnp.maximum(u[t] * COS[d] + v[t] * SIN[d], 0.0)
            push[t, d] = 0.5 * lean * lean

    zero = jnp.zeros((ROWS, LANES), jnp.float32)
    sums = [(zero, zero)] * TILES
    for f in range(F):
        for t in range(TILES):
            load(f, t).wait()
            parts = [raw[t, f * DIRS + d] for d in range(4)]
            for d in range(4, DIRS):
                parts[d % 4] = parts[d % 4] + raw[t, f * DIRS + d]
            total = (parts[0] + parts[1]) + (parts[2] + parts[3])
            energy, first = sums[t]
            sums[t] = energy + float(WEIGHT[f]) * total, first + float(WEIGHT[f] * SIGMA[f]) * total
    damps = []
    for t, (energy, first) in enumerate(sums):
        mean_sigma = first / energy
        steep = energy * mean_sigma * mean_sigma / 1.5
        damps.append(0.5 * steep * steep / mean_sigma)
        damp_ref[t] = damps[t]

    def body(f, carry):
        inverse = [geo[3, t] / (1.0 + of_freq(SIGMA, f) * damps[t]) for t in range(TILES)]
        base = pl.multiple_of(f * SPAN, SPAN)
        make_sources(raw, src0, push, inverse, f, base)
        make_packs(src0, base, f, line, up_ref, down_ref)
        return carry

    lax.fori_loop(0, CHUNKS[0], body, 0)


def rest_kernel(raw, src0, push, damp, geo, *refs):
    n = len(CHUNKS) - 1
    src, edge = refs[:2]
    ups, downs, line = refs[2 : 2 + n], refs[2 + n : 2 + 2 * n], refs[2 + 2 * n]
    at = CHUNKS[0]
    for c in range(n):
        def body(local, carry, c=c, at=at):
            f = at + local
            inverse = [geo[3, t] / (1.0 + of_freq(SIGMA, f) * damp[t]) for t in range(TILES)]
            base = pl.multiple_of((f - CHUNKS[0]) * SPAN, SPAN)
            make_sources(raw, src, push, inverse, f, base)
            make_packs(src, base, local, line, ups[c], downs[c])
            return carry

        lax.fori_loop(0, CHUNKS[c + 1], body, 0)
        at += CHUNKS[c + 1]

    def edges(d, carry):
        pairs = []
        for f in range(F):
            ref, local = (src0, f) if f < CHUNKS[0] else (src, f - CHUNKS[0])
            row = pl.ds(pl.multiple_of(local * SPAN + d * ROWS, ROWS), ROWS)
            pairs.append((ref[0, row, :], ref[1, row, :]))
        edge[pl.ds(pl.multiple_of(d * ROWS, ROWS), ROWS), :] = put_edges(pairs)
        return carry

    lax.fori_loop(0, DIRS, edges, 0, unroll=4)
    for g in range(3):
        edge[(DIRS + g) * ROWS : (DIRS + g + 1) * ROWS, :] = put_edges([(geo[g, 0], geo[g, 1])] * F)


def join_kernel(own, other, edge, up_ref, down_ref):
    lanes = own_lanes()
    for d in range(EDGES):
        rows = slice(d * ROWS, (d + 1) * ROWS)
        edge[rows, :] = jnp.where(lanes, own[rows, :], other[rows, :])
    for ref, up in ((up_ref, True), (down_ref, False)):
        for k, d0, count, row in segments(up):
            j = ROWS - k if up else k - 1
            ref[row : row + count, :] = edge[pl.ds(d0 * ROWS + j, count, stride=ROWS), :]
        for g in range(3):
            first = (DIRS + g) * ROWS + (ROWS - SUB if up else 0)
            ref[PACK + g * SUB : PACK + (g + 1) * SUB, :] = edge[first : first + SUB, :]
        ref[PACK + 3 * SUB :, :] = jnp.zeros((EDGE_ROWS - PACK - 3 * SUB, LANES), jnp.float32)


def border_kernel(own, up, down, field):
    zero = jnp.zeros((ROWS, LANES), jnp.float32)
    for s in range(SUB):
        field[s, :PAD, :] = zero
        field[s, HEIGHT - PAD :, :] = zero
    for d in range(DIRS + 1):
        row = PAD + d * PITCH - SUB
        field[0, row : row + 2 * SUB, :] = zero
    for d in range(DIRS):
        row = PAD + d * PITCH + SUB
        field[0, row : row + ROWS, :] = own[d * ROWS : (d + 1) * ROWS, :]
    halves = (up[...], down[...])
    for value, is_up in zip(halves, (True, False)):
        for k, d0, count, row in segments(is_up):
            place = PAD + d0 * PITCH + (SUB - k if is_up else SUB + ROWS + k - 1)
            field[0, pl.ds(place, count, stride=PITCH), :] = value[row : row + count]
    speed = jnp.zeros((ROWS, LANES), jnp.float32)
    for f in range(F):
        speed = jnp.where(lane_iota() >= f * STRIP, float(SPEED[f]), speed)
    coefficients = []
    for half in range(2):
        geo = []
        for g in range(3):
            mine = own[(DIRS + g) * ROWS + half * SUB : (DIRS + g) * ROWS + (half + 1) * SUB, :]
            halo = halves[half][PACK + g * SUB : PACK + (g + 1) * SUB]
            geo.append(speed * jnp.concatenate([mine, halo] if half else [halo, mine], axis=0))
        coefficients.append((geo[0], 0.5 * geo[1], 0.5 * geo[2]))
    for step in range(SUB - 1):
        for half in range(2):
            depth, sx, sy = coefficients[half]

            def load(d, shift=0):
                row = PAD + (d % DIRS) * PITCH + half * ROWS + shift
                return field[step, row : row + ROWS, :]

            for d in range(DIRS):
                west, south = COS[d] >= 0.0, SIN[d] >= 0.0
                cos, sin = abs(COS[d]), abs(SIN[d])
                now = load(d)
                up_x = pltpu.roll(now, 1 if west else LANES - 1, 1)
                up_y = load(d, -1 if south else 1)
                vt = SIN[d] * sx - COS[d] * sy
                up_t = jnp.where(vt > 0.0, load(d - 1), load(d + 1))
                moved = depth * (cos * up_x + sin * up_y - (cos + sin) * now) + jnp.abs(vt) * (up_t - now)
                row = PAD + d * PITCH + half * ROWS
                field[step + 1, row : row + ROWS, :] = now + moved


def step_kernel(first, start, *refs):
    if first:
        (src, up, down, border, geo_own, geo_up, geo_down, out, geo, field_a, field_b, turn) = refs
    else:
        (src, up, down, border, geo, _, out, token, field_a, field_b, turn) = refs
        token[...] = jnp.zeros((ROWS, LANES), jnp.float32)

    @pl.when(pl.program_id(0) == 0)
    def _():
        if first:
            for g in range(3):
                rows = slice(g * SUB, (g + 1) * SUB)
                for t in range(TILES):
                    lanes = slice(t * LANES, (t + 1) * LANES)
                    geo[g, t, :SUB] = geo_up[rows, lanes]
                    geo[g, t, SUB : SUB + ROWS] = geo_own[g, t]
                    geo[g, t, SUB + ROWS :] = geo_down[rows, lanes]
        zero = jnp.zeros((ROWS, LANES), jnp.float32)
        for t in range(TILES):
            for field in (field_a, field_b):
                field[t, :PAD, :] = zero
                field[t, HEIGHT - PAD :, :] = zero
            for d in range(DIRS + 1):
                row = PAD + d * PITCH - SUB
                field_a[t, row : row + 2 * SUB, :] = zero
        for t in range(TILES):
            for half in range(2):
                rows = slice(half * ROWS, (half + 1) * ROWS)
                sx, sy = 0.5 * geo[1, t, rows], 0.5 * geo[2, t, rows]
                for d in range(DIRS):
                    turn[t, d * PITCH + half * ROWS : d * PITCH + (half + 1) * ROWS, :] = SIN[d] * sx - COS[d] * sy

    for d in range(DIRS):
        row = PAD + d * PITCH + SUB
        for t in range(TILES):
            field_a[t, row : row + ROWS, :] = src[t, d * ROWS : (d + 1) * ROWS, :]
    for ref, is_up in ((up, True), (down, False)):
        for k, d0, count, row in segments(is_up):
            place = PAD + d0 * PITCH + (SUB - k if is_up else SUB + ROWS + k - 1)
            place = pl.ds(place, count, stride=PITCH)
            for t in range(TILES):
                field_a[t, place, :] = ref[row : row + count, t * LANES : (t + 1) * LANES]

    freq = start + pl.program_id(0)
    speed = of_freq(SPEED, freq)
    lanes = lane_iota()
    at_first, at_last = lanes == 0, lanes == LANES - 1
    to_first = LANES - (freq * STRIP + SUB - 1)
    to_last = LANES - 1 - (freq * STRIP + SUB + 2)

    def advance(step, old, new):
        last = step == SUB - 1
        for part in (SUB,) if last else (0, ROWS):
            depth = [speed * geo[0, t, part : part + ROWS] for t in range(TILES)]

            def load(d, shift=0):
                row = PAD + (d % DIRS) * PITCH + part + shift
                return [old[t, row : row + ROWS, :] for t in range(TILES)]

            before, now = load(-1), load(0)
            initial = now
            for d in range(DIRS):
                after = load(d + 1) if d < DIRS - 1 else initial
                west, south = COS[d] >= 0.0, SIN[d] >= 0.0
                cos, sin = abs(COS[d]), abs(SIN[d])
                row = PAD + d * PITCH + part
                outer = pltpu.roll(border[step, row : row + ROWS, :], to_first if west else to_last, 1)
                rolled = [pltpu.roll(x, 1 if west else LANES - 1, 1) for x in now]
                up_y = load(d, -1 if south else 1)
                for t in range(TILES):
                    if west:
                        up_x = jnp.where(at_first, rolled[t - 1] if t else outer, rolled[t])
                    else:
                        up_x = jnp.where(at_last, rolled[t + 1] if t < TILES - 1 else outer, rolled[t])
                    vt = turn[t, d * PITCH + part : d * PITCH + part + ROWS, :]
                    up_t = jnp.where(vt > 0.0, before[t], after[t])
                    moved = depth[t] * (cos * up_x + sin * up_y[t] - (cos + sin) * now[t])
                    value = now[t] + (moved + speed * jnp.abs(vt) * (up_t - now[t]))
                    if last:
                        out[d, :, t * LANES : (t + 1) * LANES] = value
                    else:
                        new[t, row : row + ROWS, :] = value
                before, now = now, after

    fields = (field_a, field_b)
    for step in range(SUB):
        advance(step, fields[step % 2], fields[(step + 1) % 2])


def after(value, *others):
    return lax.optimization_barrier((value, *others))[0]


def per_device(spectrum, wind_u, wind_v, sea_mask, depth_factor, slope_x, slope_y):
    nbins, rows, cols = spectrum.shape
    assert (nbins, rows, cols) == (F * DIRS, ROWS, TILES * LANES)
    assert lax.axis_size("pt") == 2
    f32 = jnp.float32
    shape = lambda *s: jax.ShapeDtypeStruct(s, f32)
    scratch = lambda *s: pltpu.VMEM(s, f32)
    heights = [c * PACK + (GEO if i == 0 else 0) for i, c in enumerate(CHUNKS)]
    params = pltpu.CompilerParams(vmem_limit_bytes=32 * 2**20)
    cost = pl.CostEstimate(flops=1000, bytes_accessed=1000, transcendentals=0)
    tile = (rows, LANES)

    pinned = [
        pltpu.with_memory_space_constraint(x, pltpu.HBM)
        for x in (spectrum, wind_u, wind_v, sea_mask, depth_factor, slope_x, slope_y)
    ]
    raw, src0, push, damp, geo_own, up0, down0 = pl.pallas_call(
        head_kernel,
        out_shape=[
            shape(TILES, nbins, *tile),
            shape(TILES, CHUNKS[0] * SPAN, LANES),
            shape(TILES, DIRS, *tile),
            shape(TILES, *tile),
            shape(4, TILES, *tile),
            shape(heights[0], cols),
            shape(heights[0], cols),
        ],
        in_specs=[HBM] * 7,
        out_specs=[VMEM] * 7,
        scratch_shapes=[pltpu.VMEM((rows, cols), x.dtype) for x in (wind_u, wind_v, sea_mask, depth_factor, slope_x, slope_y)]
        + [scratch(TILES, PACK, LANES), pltpu.SemaphoreType.DMA((6,)), pltpu.SemaphoreType.DMA((F, TILES))],
        compiler_params=params,
        cost_estimate=cost,
        name="head",
    )(*pinned)

    n = len(CHUNKS) - 1
    outs = pl.pallas_call(
        rest_kernel,
        out_shape=[
            shape(TILES, (F - CHUNKS[0]) * SPAN, LANES),
            shape(EDGES * rows, LANES),
            *[shape(h, cols) for h in heights[1:]] * 2,
        ],
        in_specs=[VMEM] * 5,
        out_specs=[VMEM] * (2 + 2 * n),
        scratch_shapes=[scratch(TILES, PACK, LANES)],
        compiler_params=params,
        cost_estimate=cost,
        name="rest",
    )(raw, src0, push, damp, geo_own)
    src, edge = outs[:2]
    ups, downs = [up0, *outs[2 : 2 + n]], [down0, *outs[2 + n :]]

    blocks = lax.axis_size("region") * lax.axis_size("bin")
    up_pairs = [(i, i + 1) for i in range(blocks - 1)]
    down_pairs = [(j, i) for i, j in up_pairs]
    send_up = lambda x: lax.ppermute(x, ("region", "bin"), up_pairs)
    send_down = lambda x: lax.ppermute(x, ("region", "bin"), down_pairs)

    from_south, from_north = [send_up(ups[0])], [send_down(downs[0])]
    other = lax.ppermute(edge, "pt", [(0, 1), (1, 0)])
    edge, edge_up, edge_down = pl.pallas_call(
        join_kernel,
        out_shape=[shape(EDGES * rows, LANES), shape(EDGE_ROWS, LANES), shape(EDGE_ROWS, LANES)],
        in_specs=[VMEM] * 2,
        out_specs=[VMEM] * 3,
        compiler_params=params,
        cost_estimate=cost,
        name="join",
    )(edge, other)
    edge_south, edge_north = send_up(edge_up), send_down(edge_down)
    border = pl.pallas_call(
        border_kernel,
        out_shape=shape(SUB, HEIGHT, LANES),
        in_specs=[VMEM] * 3,
        out_specs=VMEM,
        compiler_params=params,
        cost_estimate=cost,
        name="border",
    )(edge, edge_south, edge_north)
    token = (edge_south, edge_north)

    block = pl.BlockSpec
    start, geo, result = 0, None, None
    for c, count in enumerate(CHUNKS):
        first = c == 0
        at = start
        if c + 1 < n + 1:
            from_south.append(send_up(after(ups[c + 1], *token)))
            from_north.append(send_down(after(downs[c + 1], *token)))
        source_at = at - (0 if first else CHUNKS[0])
        operands = [src0 if first else src, from_south[c], from_north[c], border]
        in_specs = [
            block((TILES, SPAN, LANES), lambda i, at=source_at: (0, at + i, 0)),
            block((PACK, cols), lambda i: (i, 0)),
            block((PACK, cols), lambda i: (i, 0)),
            block((SUB, HEIGHT, LANES), lambda i: (0, 0, 0)),
        ]
        geo_shape = (3, TILES, PITCH, LANES)
        geo_block = block(geo_shape, lambda i: (0, 0, 0, 0))
        out_shape = [shape(nbins, rows, cols)]
        out_specs = [block((DIRS, rows, cols), lambda i, at=at: (at + i, 0, 0))]
        aliases = {}
        if first:
            row = count * PACK // GEO
            operands += [geo_own, from_south[c], from_north[c]]
            in_specs += [
                block((4, TILES, *tile), lambda i: (0, 0, 0, 0)),
                block((GEO, cols), lambda i, g=row: (g, 0)),
                block((GEO, cols), lambda i, g=row: (g, 0)),
            ]
            out_shape.append(shape(*geo_shape))
            out_specs.append(geo_block)
        else:
            operands += [geo, result]
            in_specs += [geo_block, ANY]
            out_shape.append(shape(*tile))
            out_specs.append(block(tile, lambda i: (0, 0)))
            aliases = {len(operands) - 1: 0}

        def kernel(*refs, first=first, at=at):
            step_kernel(first, at, *refs)

        result, last = pl.pallas_call(
            kernel,
            grid=(count,),
            out_shape=out_shape,
            in_specs=in_specs,
            out_specs=out_specs,
            scratch_shapes=[scratch(TILES, HEIGHT, LANES)] * 2 + [scratch(TILES, DIRS * PITCH, LANES)],
            input_output_aliases=aliases,
            compiler_params=params,
            cost_estimate=pl.CostEstimate(flops=1000, bytes_accessed=1000, transcendentals=0),
            name=f"steps_{c}",
        )(*operands)
        token = (last,)
        if first:
            geo = last
        start += count
    return result


def solution(mesh):
    in_specs = (
        P("ens", ("region", "bin"), "pt"),
        P(("ens", "region", "bin"), "pt"),
        P(("ens", "region", "bin"), "pt"),
        P("region", "pt"),
        P("region", "pt"),
        P("region", "pt"),
        P("region", "pt"),
    )
    out_specs = P("ens", ("region", "bin"), "pt")
    return jax.shard_map(
        per_device, mesh=mesh, in_specs=in_specs, out_specs=out_specs, check_vma=False
    )
```

```python
import math

import jax
import jax.numpy as jnp
import numpy as np
from jax import lax
from jax.experimental import pallas as pl
from jax.experimental.pallas import tpu as pltpu
from jax.sharding import PartitionSpec as P

F = 12
DIRS = 36
SUB = 4
ROWS = 8
LANES = 128
TILES = 2
HALF = DIRS // 2
SENT = [HALF - 1 + 2 * (SUB - k) for k in range(1, SUB + 1)]
PACK = sum(SENT)
GEO = 16
CHUNKS = (4, 2, 4, 2)
STRIP = 2 * SUB + 2
EDGES = DIRS + 3
TAIL = 48
PITCH = ROWS + 2 * SUB
PAD = 8
HEIGHT = DIRS * PITCH + 2 * PAD
SPAN = DIRS * ROWS

SIGMA = 0.6 * 1.1 ** np.arange(F, dtype=np.float64)
WEIGHT = SIGMA / (DIRS * SIGMA.sum())


def quarter_exact(fn):
    values = np.array([fn(2.0 * math.pi * d / DIRS) for d in range(DIRS)])
    values[np.abs(values) < 1e-9] = 0.0
    return [float(x) for x in values]


COS = quarter_exact(math.cos)
SIN = quarter_exact(math.sin)
SPEED = 0.27 / SIGMA


def of_freq(values, f):
    if isinstance(f, int):
        return float(values[f])
    out = jnp.float32(values[0])
    for i in range(1, F):
        out = jnp.where(f == i, jnp.float32(values[i]), out)
    return out


HBM = pl.BlockSpec(memory_space=pltpu.HBM)
VMEM = pl.BlockSpec(memory_space=pltpu.VMEM)
ANY = pl.BlockSpec(memory_space=pl.ANY)


def segments(up):
    out, row = [], 0
    for k in range(1, SUB + 1):
        low = 1 - (SUB - k) + (0 if up else HALF)
        left, at = SENT[k - 1], low
        while left > 0:
            first = at % DIRS
            count = min(left, DIRS - first)
            out.append((k, first, count, row))
            row, at, left = row + count, at + count, left - count
    return out


def lane_iota():
    return lax.broadcasted_iota(jnp.int32, (ROWS, LANES), 1)


def own_lanes():
    own = jnp.zeros((ROWS, LANES), jnp.bool_)
    for f in range(F):
        own = own | (lane_iota() == f * STRIP + SUB) | (lane_iota() == f * STRIP + SUB + 1)
    return own


def put_edges(pairs):
    lanes = lane_iota()
    packed = jnp.zeros((ROWS, LANES), jnp.float32)
    for f, (first_tile, last_tile) in enumerate(pairs):
        ends = jnp.where(lanes < LANES // 2, first_tile, last_tile)
        at = f * STRIP
        packed = jnp.where(lanes >= at, pltpu.roll(ends, (at + SUB) % LANES, 1), packed)
        packed = jnp.where(lanes >= at + SUB + 1, pltpu.roll(ends, (at + SUB + 2) % LANES, 1), packed)
    return packed


def split(value):
    return value[:, :LANES], value[:, LANES:]


def make_sources(raw, src, push, inverse, f, base):
    sig = of_freq(SIGMA, f)
    for t in range(TILES):
        for d in range(DIRS):
            grown = raw[t, f * DIRS + d] * (1.0 + sig * push[t, d])
            row = base + d * ROWS
            src[t, pl.ds(row, ROWS), :] = grown * inverse[t]


def make_packs(src, base, local, up_ref, down_ref):
    for ref, up in ((up_ref, True), (down_ref, False)):
        for k, d0, count, row in segments(up):
            j = ROWS - k if up else k - 1
            for t in range(TILES):
                ref[t, pl.ds(local * PACK + row, count), :] = src[t, pl.ds(base + d0 * ROWS + j, count, stride=ROWS), :]


def head_kernel(
    spec, u_hbm, v_hbm, mask_hbm, depth_hbm, sx_hbm, sy_hbm,
    raw, src0, push, damp_ref, geo, up_ref, down_ref,
    u_ref, v_ref, mask_ref, depth_ref, sx_ref, sy_ref, small_sem, in_sem,
):
    off = pl.multiple_of(lax.axis_index("bin") * ROWS, ROWS)
    own = pl.ds(off, ROWS)
    small = [
        pltpu.make_async_copy(a, b, small_sem.at[i])
        for i, (a, b) in enumerate(
            (
                (u_hbm, u_ref),
                (v_hbm, v_ref),
                (mask_hbm.at[own], mask_ref),
                (depth_hbm.at[own], depth_ref),
                (sx_hbm.at[own], sx_ref),
                (sy_hbm.at[own], sy_ref),
            )
        )
    ]

    def load(f, t):
        return pltpu.make_async_copy(
            spec.at[pl.ds(f * DIRS, DIRS), :, pl.ds(t * LANES, LANES)],
            raw.at[t, pl.ds(f * DIRS, DIRS)],
            in_sem.at[f, t],
        )

    for copy in small:
        copy.start()
    for f in range(F):
        for t in range(TILES):
            load(f, t).start()
    for copy in small:
        copy.wait()

    mask = mask_ref[...].astype(jnp.float32)
    fields = (depth_ref[...] * mask, sx_ref[...] * mask, sy_ref[...] * mask)
    tail = CHUNKS[0] * PACK
    for g in range(3):
        for t, tile in enumerate(split(fields[g])):
            geo[g, t] = tile
        rows = slice(tail + g * SUB, tail + (g + 1) * SUB)
        for t, tile in enumerate(split(fields[g])):
            up_ref[t, rows, :] = tile[ROWS - SUB :, :]
            down_ref[t, rows, :] = tile[:SUB, :]
    for ref in (up_ref, down_ref):
        for t in range(TILES):
            ref[t, tail + 3 * SUB :, :] = jnp.zeros((GEO - 3 * SUB, LANES), jnp.float32)
    for t, tile in enumerate(split(mask)):
        geo[3, t] = tile
    u, v = split(u_ref[...]), split(v_ref[...])
    for d in range(DIRS):
        for t in range(TILES):
            lean = jnp.maximum(u[t] * COS[d] + v[t] * SIN[d], 0.0)
            push[t, d] = 0.5 * lean * lean

    zero = jnp.zeros((ROWS, LANES), jnp.float32)
    sums = [(zero, zero)] * TILES
    for f in range(F):
        for t in range(TILES):
            load(f, t).wait()
            parts = [raw[t, f * DIRS + d] for d in range(4)]
            for d in range(4, DIRS):
                parts[d % 4] = parts[d % 4] + raw[t, f * DIRS + d]
            total = (parts[0] + parts[1]) + (parts[2] + parts[3])
            energy, first = sums[t]
            sums[t] = energy + float(WEIGHT[f]) * total, first + float(WEIGHT[f] * SIGMA[f]) * total
    damps = []
    for t, (energy, first) in enumerate(sums):
        mean_sigma = first / energy
        steep = energy * mean_sigma * mean_sigma / 1.5
        damps.append(0.5 * steep * steep / mean_sigma)
        damp_ref[t] = damps[t]

    def body(f, carry):
        inverse = [geo[3, t] / (1.0 + of_freq(SIGMA, f) * damps[t]) for t in range(TILES)]
        base = pl.multiple_of(f * SPAN, SPAN)
        make_sources(raw, src0, push, inverse, f, base)
        make_packs(src0, base, f, up_ref, down_ref)
        return carry

    lax.fori_loop(0, CHUNKS[0], body, 0)


def rest_kernel(raw, src0, push, damp, geo, *refs):
    n = len(CHUNKS) - 1
    src, edge = refs[:2]
    ups, downs = refs[2 : 2 + n], refs[2 + n :]
    at = CHUNKS[0]
    for c in range(n):
        def body(local, carry, c=c, at=at):
            f = at + local
            inverse = [geo[3, t] / (1.0 + of_freq(SIGMA, f) * damp[t]) for t in range(TILES)]
            base = pl.multiple_of((f - CHUNKS[0]) * SPAN, SPAN)
            make_sources(raw, src, push, inverse, f, base)
            make_packs(src, base, local, ups[c], downs[c])
            return carry

        lax.fori_loop(0, CHUNKS[c + 1], body, 0)
        at += CHUNKS[c + 1]

    def edges(d, carry):
        pairs = []
        for f in range(F):
            ref, local = (src0, f) if f < CHUNKS[0] else (src, f - CHUNKS[0])
            row = pl.ds(pl.multiple_of(local * SPAN + d * ROWS, ROWS), ROWS)
            pairs.append((ref[0, row, :], ref[1, row, :]))
        edge[pl.ds(pl.multiple_of(d * ROWS, ROWS), ROWS), :] = put_edges(pairs)
        return carry

    lax.fori_loop(0, DIRS, edges, 0, unroll=4)
    for g in range(3):
        edge[(DIRS + g) * ROWS : (DIRS + g + 1) * ROWS, :] = put_edges([(geo[g, 0], geo[g, 1])] * F)


def join_kernel(own, other, up_in, down_in, edge, up_out, down_out, tails, sem):
    lanes = own_lanes()
    for d in range(EDGES):
        rows = slice(d * ROWS, (d + 1) * ROWS)
        edge[rows, :] = jnp.where(lanes, own[rows, :], other[rows, :])
    copies = []
    for i, (out, up) in enumerate(((up_out, True), (down_out, False))):
        pieces = [
            (row, count, pl.ds(d0 * ROWS + (ROWS - k if up else k - 1), count, stride=ROWS))
            for k, d0, count, row in segments(up)
        ]
        for g in range(3):
            pieces.append((PACK + g * SUB, SUB, pl.ds((DIRS + g) * ROWS + (ROWS - SUB if up else 0), SUB)))
        for row, count, place in pieces:
            value, at = edge[place, :], 0
            while at < count:
                half, inner = divmod(row + at, TAIL)
                size = min(count - at, TAIL - inner)
                tails[i, half, inner : inner + size, :] = value[at : at + size]
                at += size
        rest = 2 * TAIL - PACK - 3 * SUB
        tails[i, 1, TAIL - rest :, :] = jnp.zeros((rest, LANES), jnp.float32)
        copies.append(
            pltpu.make_async_copy(tails.at[i], out.at[:, pl.ds(CHUNKS[1] * PACK, TAIL)], sem.at[i])
        )
        copies[-1].start()
    for copy in copies:
        copy.wait()


def border_kernel(own, up, down, field):
    zero = jnp.zeros((ROWS, LANES), jnp.float32)
    for s in range(SUB):
        field[s, :PAD, :] = zero
        field[s, HEIGHT - PAD :, :] = zero
    for d in range(DIRS + 1):
        row = PAD + d * PITCH - SUB
        field[0, row : row + 2 * SUB, :] = zero
    for d in range(DIRS):
        row = PAD + d * PITCH + SUB
        field[0, row : row + ROWS, :] = own[d * ROWS : (d + 1) * ROWS, :]
    tail = CHUNKS[1] * PACK
    halves = [
        jnp.concatenate([ref[0, tail : tail + TAIL, :], ref[1, tail : tail + TAIL, :]], axis=0)
        for ref in (up, down)
    ]
    for value, is_up in zip(halves, (True, False)):
        for k, d0, count, row in segments(is_up):
            place = PAD + d0 * PITCH + (SUB - k if is_up else SUB + ROWS + k - 1)
            field[0, pl.ds(place, count, stride=PITCH), :] = value[row : row + count]
    speed = jnp.zeros((ROWS, LANES), jnp.float32)
    for f in range(F):
        speed = jnp.where(lane_iota() >= f * STRIP, float(SPEED[f]), speed)
    coefficients = []
    for half in range(2):
        geo = []
        for g in range(3):
            mine = own[(DIRS + g) * ROWS + half * SUB : (DIRS + g) * ROWS + (half + 1) * SUB, :]
            halo = halves[half][PACK + g * SUB : PACK + (g + 1) * SUB]
            geo.append(speed * jnp.concatenate([mine, halo] if half else [halo, mine], axis=0))
        coefficients.append((geo[0], 0.5 * geo[1], 0.5 * geo[2]))
    for step in range(SUB - 1):
        for half in range(2):
            depth, sx, sy = coefficients[half]

            def load(d, shift=0):
                row = PAD + (d % DIRS) * PITCH + half * ROWS + shift
                return field[step, row : row + ROWS, :]

            for d in range(DIRS):
                west, south = COS[d] >= 0.0, SIN[d] >= 0.0
                cos, sin = abs(COS[d]), abs(SIN[d])
                now = load(d)
                up_x = pltpu.roll(now, 1 if west else LANES - 1, 1)
                up_y = load(d, -1 if south else 1)
                vt = SIN[d] * sx - COS[d] * sy
                up_t = jnp.where(vt > 0.0, load(d - 1), load(d + 1))
                moved = depth * (cos * up_x + sin * up_y - (cos + sin) * now) + jnp.abs(vt) * (up_t - now)
                row = PAD + d * PITCH + half * ROWS
                field[step + 1, row : row + ROWS, :] = now + moved


def step_kernel(first, start, count, source_at, *refs):
    if first:
        src, up, down, border, geo_own, out, geo, field_a, field_b, turn, done, sem = refs
        tail = count * PACK
        for g in range(3):
            rows = slice(tail + g * SUB, tail + (g + 1) * SUB)
            for t in range(TILES):
                geo[g, t, :SUB] = up[t, rows, :]
                geo[g, t, SUB : SUB + ROWS] = geo_own[g, t]
                geo[g, t, SUB + ROWS :] = down[t, rows, :]
    else:
        src, up, down, border, geo, _, out, field_a, field_b, turn, done, sem = refs
    zero = jnp.zeros((ROWS, LANES), jnp.float32)
    for t in range(TILES):
        for field in (field_a, field_b):
            field[t, :PAD, :] = zero
            field[t, HEIGHT - PAD :, :] = zero
        for d in range(DIRS + 1):
            row = PAD + d * PITCH - SUB
            field_a[t, row : row + 2 * SUB, :] = zero
        for half in range(2):
            rows = slice(half * ROWS, (half + 1) * ROWS)
            sx, sy = 0.5 * geo[1, t, rows], 0.5 * geo[2, t, rows]
            for d in range(DIRS):
                turn[t, d * PITCH + half * ROWS : d * PITCH + (half + 1) * ROWS, :] = SIN[d] * sx - COS[d] * sy
    lanes = lane_iota()
    at_first, at_last = lanes == 0, lanes == LANES - 1
    quarter = DIRS // 4

    def put(i, q):
        slot = lax.rem(i, 2)
        return pltpu.make_async_copy(
            done.at[slot, pl.ds(q * quarter, quarter)],
            out.at[pl.ds((start + i) * DIRS + q * quarter, quarter)],
            sem.at[slot, q],
        )

    def frequency(i, carry):
        base = pl.multiple_of((source_at + i) * SPAN, SPAN)
        for d in range(DIRS):
            row = PAD + d * PITCH + SUB
            for t in range(TILES):
                field_a[t, row : row + ROWS, :] = src[t, pl.ds(base + d * ROWS, ROWS), :]
        for ref, is_up in ((up, True), (down, False)):
            for k, d0, number, row in segments(is_up):
                place = PAD + d0 * PITCH + (SUB - k if is_up else SUB + ROWS + k - 1)
                place = pl.ds(place, number, stride=PITCH)
                for t in range(TILES):
                    field_a[t, place, :] = ref[t, pl.ds(i * PACK + row, number), :]

        freq = start + i
        speed = of_freq(SPEED, freq)
        to_first = LANES - (freq * STRIP + SUB - 1)
        to_last = LANES - 1 - (freq * STRIP + SUB + 2)

        @pl.when(i >= 2)
        def _():
            for q in range(4):
                put(i - 2, q).wait()

        def advance(step, old, new):
            last = step == SUB - 1
            for part in (SUB,) if last else (0, ROWS):
                depth = [speed * geo[0, t, part : part + ROWS] for t in range(TILES)]

                def load(d, shift=0):
                    row = PAD + (d % DIRS) * PITCH + part + shift
                    return [old[t, row : row + ROWS, :] for t in range(TILES)]

                before, now = load(-1), load(0)
                initial = now
                for d in range(DIRS):
                    after = load(d + 1) if d < DIRS - 1 else initial
                    west, south = COS[d] >= 0.0, SIN[d] >= 0.0
                    cos, sin = abs(COS[d]), abs(SIN[d])
                    row = PAD + d * PITCH + part
                    outer = pltpu.roll(border[step, row : row + ROWS, :], to_first if west else to_last, 1)
                    rolled = [pltpu.roll(x, 1 if west else LANES - 1, 1) for x in now]
                    up_y = load(d, -1 if south else 1)
                    for t in range(TILES):
                        if west:
                            up_x = jnp.where(at_first, rolled[t - 1] if t else outer, rolled[t])
                        else:
                            up_x = jnp.where(at_last, rolled[t + 1] if t < TILES - 1 else outer, rolled[t])
                        vt = turn[t, d * PITCH + part : d * PITCH + part + ROWS, :]
                        up_t = jnp.where(vt > 0.0, before[t], after[t])
                        moved = depth[t] * (cos * up_x + sin * up_y[t] - (cos + sin) * now[t])
                        value = now[t] + (moved + speed * jnp.abs(vt) * (up_t - now[t]))
                        if last:
                            done[lax.rem(i, 2), d, :, t * LANES : (t + 1) * LANES] = value
                        else:
                            new[t, row : row + ROWS, :] = value
                    before, now = now, after
                    if last and d % quarter == quarter - 1:
                        put(i, d // quarter).start()

        fields = (field_a, field_b)
        for step in range(SUB):
            advance(step, fields[step % 2], fields[(step + 1) % 2])
        return carry

    lax.fori_loop(0, count, frequency, 0)
    for i in range(max(count - 2, 0), count):
        for q in range(4):
            put(i, q).wait()


def after(value, *others):
    return lax.optimization_barrier((value, *others))[0]


def per_device(spectrum, wind_u, wind_v, sea_mask, depth_factor, slope_x, slope_y):
    nbins, rows, cols = spectrum.shape
    assert (nbins, rows, cols) == (F * DIRS, ROWS, TILES * LANES)
    assert lax.axis_size("pt") == 2
    f32 = jnp.float32
    shape = lambda *s: jax.ShapeDtypeStruct(s, f32)
    scratch = lambda *s: pltpu.VMEM(s, f32)
    heights = [c * PACK + (GEO, TAIL, 0, 0)[min(i, 2)] for i, c in enumerate(CHUNKS)]
    params = pltpu.CompilerParams(vmem_limit_bytes=32 * 2**20)
    cost = pl.CostEstimate(flops=1000, bytes_accessed=1000, transcendentals=0)
    tile = (rows, LANES)

    pinned = [
        pltpu.with_memory_space_constraint(x, pltpu.HBM)
        for x in (spectrum, wind_u, wind_v, sea_mask, depth_factor, slope_x, slope_y)
    ]
    raw, src0, push, damp, geo_own, up0, down0 = pl.pallas_call(
        head_kernel,
        out_shape=[
            shape(TILES, nbins, *tile),
            shape(TILES, CHUNKS[0] * SPAN, LANES),
            shape(TILES, DIRS, *tile),
            shape(TILES, *tile),
            shape(4, TILES, *tile),
            shape(TILES, heights[0], LANES),
            shape(TILES, heights[0], LANES),
        ],
        in_specs=[HBM] * 7,
        out_specs=[VMEM] * 7,
        scratch_shapes=[pltpu.VMEM((rows, cols), x.dtype) for x in (wind_u, wind_v, sea_mask, depth_factor, slope_x, slope_y)]
        + [pltpu.SemaphoreType.DMA((6,)), pltpu.SemaphoreType.DMA((F, TILES))],
        compiler_params=params,
        cost_estimate=cost,
        name="head",
    )(*pinned)

    n = len(CHUNKS) - 1
    outs = pl.pallas_call(
        rest_kernel,
        out_shape=[
            shape(TILES, (F - CHUNKS[0]) * SPAN, LANES),
            shape(EDGES * rows, LANES),
            *[shape(TILES, h, LANES) for h in heights[1:]] * 2,
        ],
        in_specs=[VMEM] * 5,
        out_specs=[VMEM] * (2 + 2 * n),
        compiler_params=params,
        cost_estimate=cost,
        name="rest",
    )(raw, src0, push, damp, geo_own)
    src, edge = outs[:2]
    ups, downs = [up0, *outs[2 : 2 + n]], [down0, *outs[2 + n :]]

    blocks = lax.axis_size("region") * lax.axis_size("bin")
    up_pairs = [(i, i + 1) for i in range(blocks - 1)]
    down_pairs = [(j, i) for i, j in up_pairs]
    send_up = lambda x: lax.ppermute(x, ("region", "bin"), up_pairs)
    send_down = lambda x: lax.ppermute(x, ("region", "bin"), down_pairs)

    from_south, from_north = [send_up(ups[0])], [send_down(downs[0])]
    other = lax.ppermute(edge, "pt", [(0, 1), (1, 0)])
    edge, ups[1], downs[1] = pl.pallas_call(
        join_kernel,
        out_shape=[shape(EDGES * rows, LANES), shape(TILES, heights[1], LANES), shape(TILES, heights[1], LANES)],
        in_specs=[VMEM, VMEM, ANY, ANY],
        out_specs=[VMEM, ANY, ANY],
        scratch_shapes=[scratch(2, TILES, TAIL, LANES), pltpu.SemaphoreType.DMA((2,))],
        input_output_aliases={2: 1, 3: 2},
        compiler_params=params,
        cost_estimate=cost,
        name="join",
    )(edge, other, ups[1], downs[1])
    wait = (from_south[0], from_north[0])
    from_south += [send_up(ups[1]), send_up(after(ups[2], *wait))]
    from_north += [send_down(downs[1]), send_down(after(downs[2], *wait))]
    border = pl.pallas_call(
        border_kernel,
        out_shape=shape(SUB, HEIGHT, LANES),
        in_specs=[VMEM] * 3,
        out_specs=VMEM,
        compiler_params=params,
        cost_estimate=cost,
        name="border",
    )(edge, from_south[1], from_north[1])


    start, geo, result = 0, None, None
    for c, count in enumerate(CHUNKS):
        first = c == 0
        operands = [src0 if first else src, from_south[c], from_north[c], border]
        in_specs = [VMEM] * 5
        out_shape = [shape(nbins, rows, cols)]
        aliases = {}
        if first:
            operands.append(geo_own)
            out_shape.append(shape(3, TILES, PITCH, LANES))
        else:
            operands += [geo, result]
            in_specs.append(ANY)
            aliases = {len(operands) - 1: 0}

        def kernel(*refs, first=first, start=start, count=count):
            step_kernel(first, start, count, start - (0 if first else CHUNKS[0]), *refs)

        outs = pl.pallas_call(
            kernel,
            out_shape=out_shape,
            in_specs=in_specs,
            out_specs=[ANY, VMEM][: len(out_shape)],
            scratch_shapes=[scratch(TILES, HEIGHT, LANES)] * 2
            + [scratch(TILES, DIRS * PITCH, LANES), scratch(2, DIRS, rows, cols), pltpu.SemaphoreType.DMA((2, 4))],
            input_output_aliases=aliases,
            compiler_params=params,
            cost_estimate=cost,
            name=f"steps_{c}",
        )(*operands)
        result = outs[0]
        if first:
            geo = outs[1]
            for later in range(3, len(CHUNKS)):
                from_south.append(send_up(after(ups[later], geo)))
                from_north.append(send_down(after(downs[later], geo)))
        start += count
    return result


def solution(mesh):
    in_specs = (
        P("ens", ("region", "bin"), "pt"),
        P(("ens", "region", "bin"), "pt"),
        P(("ens", "region", "bin"), "pt"),
        P("region", "pt"),
        P("region", "pt"),
        P("region", "pt"),
        P("region", "pt"),
    )
    out_specs = P("ens", ("region", "bin"), "pt")
    return jax.shard_map(
        per_device, mesh=mesh, in_specs=in_specs, out_specs=out_specs, check_vma=False
    )
```

```python
import functools
import math

import jax
import jax.numpy as jnp
import numpy as np
from jax import lax
from jax.experimental import pallas as pl
from jax.experimental.pallas import tpu as pltpu
from jax.sharding import PartitionSpec as P

F = 12
DIRS = 36
SUB = 4
ROWS = 8
LANES = 128
TILES = 2
HALF = DIRS // 2
SENT = [HALF - 1 + 2 * (SUB - k) for k in range(1, SUB + 1)]
PACK = sum(SENT)
GEO = 16
CHUNKS = (4, 2, 4, 2)
STRIP = 2 * SUB + 2
EDGES = DIRS + 3
TAIL = 48
PITCH = ROWS + 2 * SUB
PAD = 8
HEIGHT = DIRS * PITCH + 2 * PAD
SPAN = DIRS * ROWS

SIGMA = 0.6 * 1.1 ** np.arange(F, dtype=np.float64)
WEIGHT = SIGMA / (DIRS * SIGMA.sum())


def quarter_exact(fn):
    values = np.array([fn(2.0 * math.pi * d / DIRS) for d in range(DIRS)])
    values[np.abs(values) < 1e-9] = 0.0
    return [float(x) for x in values]


COS = quarter_exact(math.cos)
SIN = quarter_exact(math.sin)
SPEED = 0.27 / SIGMA


def of_freq(values, f):
    if isinstance(f, int):
        return float(values[f])
    out = jnp.float32(values[0])
    for i in range(1, F):
        out = jnp.where(f == i, jnp.float32(values[i]), out)
    return out


HBM = pl.BlockSpec(memory_space=pltpu.HBM)
VMEM = pl.BlockSpec(memory_space=pltpu.VMEM)
ANY = pl.BlockSpec(memory_space=pl.ANY)


def segments(up):
    out, row = [], 0
    for k in range(1, SUB + 1):
        low = 1 - (SUB - k) + (0 if up else HALF)
        left, at = SENT[k - 1], low
        while left > 0:
            first = at % DIRS
            count = min(left, DIRS - first)
            out.append((k, first, count, row))
            row, at, left = row + count, at + count, left - count
    return out


def lane_iota():
    return lax.broadcasted_iota(jnp.int32, (ROWS, LANES), 1)


def own_lanes():
    own = jnp.zeros((ROWS, LANES), jnp.bool_)
    for f in range(F):
        own = own | (lane_iota() == f * STRIP + SUB) | (lane_iota() == f * STRIP + SUB + 1)
    return own


def put_edges(pairs):
    lanes = lane_iota()
    packed = jnp.zeros((ROWS, LANES), jnp.float32)
    for f, (first_tile, last_tile) in enumerate(pairs):
        ends = jnp.where(lanes < LANES // 2, first_tile, last_tile)
        at = f * STRIP
        packed = jnp.where(lanes >= at, pltpu.roll(ends, (at + SUB) % LANES, 1), packed)
        packed = jnp.where(lanes >= at + SUB + 1, pltpu.roll(ends, (at + SUB + 2) % LANES, 1), packed)
    return packed


def is_even(bins):
    return lax.rem(lax.axis_index("region") * bins + lax.axis_index("bin"), 2) == 0


def by_parity(even, run):
    pl.when(even)(lambda: run(True))
    pl.when(jnp.logical_not(even))(lambda: run(False))


def split(value):
    return value[:, :LANES], value[:, LANES:]


def make_sources(raw, src, push, inverse, f, base):
    sig = of_freq(SIGMA, f)
    for t in range(TILES):
        for d in range(DIRS):
            grown = raw[t, f * DIRS + d] * (1.0 + sig * push[t, d])
            row = base + d * ROWS
            src[t, pl.ds(row, ROWS), :] = grown * inverse[t]


def make_packs(even, src, base, local, near, far):
    def run(north_near):
        for ref, up in ((near, north_near), (far, not north_near)):
            for k, d0, count, row in segments(up):
                j = ROWS - k if up else k - 1
                for t in range(TILES):
                    value = src[t, pl.ds(base + d0 * ROWS + j, count, stride=ROWS), :]
                    ref[t, pl.ds(local * PACK + row, count), :] = value

    by_parity(even, run)


def head_kernel(
    bins, spec, u_hbm, v_hbm, mask_hbm, depth_hbm, sx_hbm, sy_hbm,
    raw, src0, push, damp_ref, geo, near, far,
    u_ref, v_ref, mask_ref, depth_ref, sx_ref, sy_ref, small_sem, in_sem,
):
    even = is_even(bins)
    off = pl.multiple_of(lax.axis_index("bin") * ROWS, ROWS)
    own = pl.ds(off, ROWS)
    small = [
        pltpu.make_async_copy(a, b, small_sem.at[i])
        for i, (a, b) in enumerate(
            (
                (u_hbm, u_ref),
                (v_hbm, v_ref),
                (mask_hbm.at[own], mask_ref),
                (depth_hbm.at[own], depth_ref),
                (sx_hbm.at[own], sx_ref),
                (sy_hbm.at[own], sy_ref),
            )
        )
    ]

    def load(f, t):
        return pltpu.make_async_copy(
            spec.at[pl.ds(f * DIRS, DIRS), :, pl.ds(t * LANES, LANES)],
            raw.at[t, pl.ds(f * DIRS, DIRS)],
            in_sem.at[f, t],
        )

    for copy in small:
        copy.start()
    for f in range(F):
        for t in range(TILES):
            load(f, t).start()
    for copy in small:
        copy.wait()

    mask = mask_ref[...].astype(jnp.float32)
    fields = (depth_ref[...] * mask, sx_ref[...] * mask, sy_ref[...] * mask)
    tail = CHUNKS[0] * PACK
    for g in range(3):
        for t, tile in enumerate(split(fields[g])):
            geo[g, t] = tile
        rows = slice(tail + g * SUB, tail + (g + 1) * SUB)
        for t, tile in enumerate(split(fields[g])):
            near[t, rows, :] = jnp.where(even, tile[ROWS - SUB :, :], tile[:SUB, :])
            far[t, rows, :] = jnp.where(even, tile[:SUB, :], tile[ROWS - SUB :, :])
    for ref in (near, far):
        for t in range(TILES):
            ref[t, tail + 3 * SUB :, :] = jnp.zeros((GEO - 3 * SUB, LANES), jnp.float32)
    for t, tile in enumerate(split(mask)):
        geo[3, t] = tile
    u, v = split(u_ref[...]), split(v_ref[...])
    for d in range(DIRS):
        for t in range(TILES):
            lean = jnp.maximum(u[t] * COS[d] + v[t] * SIN[d], 0.0)
            push[t, d] = 0.5 * lean * lean

    zero = jnp.zeros((ROWS, LANES), jnp.float32)
    sums = [(zero, zero)] * TILES
    for f in range(F):
        for t in range(TILES):
            load(f, t).wait()
            parts = [raw[t, f * DIRS + d] for d in range(4)]
            for d in range(4, DIRS):
                parts[d % 4] = parts[d % 4] + raw[t, f * DIRS + d]
            total = (parts[0] + parts[1]) + (parts[2] + parts[3])
            energy, first = sums[t]
            sums[t] = energy + float(WEIGHT[f]) * total, first + float(WEIGHT[f] * SIGMA[f]) * total
    damps = []
    for t, (energy, first) in enumerate(sums):
        mean_sigma = first / energy
        steep = energy * mean_sigma * mean_sigma / 1.5
        damps.append(0.5 * steep * steep / mean_sigma)
        damp_ref[t] = damps[t]

    def body(f, carry):
        inverse = [geo[3, t] / (1.0 + of_freq(SIGMA, f) * damps[t]) for t in range(TILES)]
        base = pl.multiple_of(f * SPAN, SPAN)
        make_sources(raw, src0, push, inverse, f, base)
        make_packs(even, src0, base, f, near, far)
        return carry

    lax.fori_loop(0, CHUNKS[0], body, 0)


def rest_kernel(bins, raw, src0, push, damp, geo, *refs):
    n = len(CHUNKS) - 1
    src, edge = refs[:2]
    nears, fars = refs[2 : 2 + n], refs[2 + n :]
    even = is_even(bins)
    at = CHUNKS[0]
    for c in range(n):
        def body(local, carry, c=c, at=at):
            f = at + local
            inverse = [geo[3, t] / (1.0 + of_freq(SIGMA, f) * damp[t]) for t in range(TILES)]
            base = pl.multiple_of((f - CHUNKS[0]) * SPAN, SPAN)
            make_sources(raw, src, push, inverse, f, base)
            make_packs(even, src, base, local, nears[c], fars[c])
            return carry

        lax.fori_loop(0, CHUNKS[c + 1], body, 0)
        at += CHUNKS[c + 1]

    def edges(d, carry):
        pairs = []
        for f in range(F):
            ref, local = (src0, f) if f < CHUNKS[0] else (src, f - CHUNKS[0])
            row = pl.ds(pl.multiple_of(local * SPAN + d * ROWS, ROWS), ROWS)
            pairs.append((ref[0, row, :], ref[1, row, :]))
        edge[pl.ds(pl.multiple_of(d * ROWS, ROWS), ROWS), :] = put_edges(pairs)
        return carry

    lax.fori_loop(0, DIRS, edges, 0, unroll=4)
    for g in range(3):
        edge[(DIRS + g) * ROWS : (DIRS + g + 1) * ROWS, :] = put_edges([(geo[g, 0], geo[g, 1])] * F)


def join_kernel(bins, own, other, near_in, far_in, edge, near, far, tails, sem):
    lanes = own_lanes()
    for d in range(EDGES):
        rows = slice(d * ROWS, (d + 1) * ROWS)
        edge[rows, :] = jnp.where(lanes, own[rows, :], other[rows, :])
    for i, up in enumerate((True, False)):
        pieces = [
            (row, count, pl.ds(d0 * ROWS + (ROWS - k if up else k - 1), count, stride=ROWS))
            for k, d0, count, row in segments(up)
        ]
        for g in range(3):
            pieces.append((PACK + g * SUB, SUB, pl.ds((DIRS + g) * ROWS + (ROWS - SUB if up else 0), SUB)))
        for row, count, place in pieces:
            value, at = edge[place, :], 0
            while at < count:
                half, inner = divmod(row + at, TAIL)
                size = min(count - at, TAIL - inner)
                tails[i, half, inner : inner + size, :] = value[at : at + size]
                at += size
        rest = 2 * TAIL - PACK - 3 * SUB
        tails[i, 1, TAIL - rest :, :] = jnp.zeros((rest, LANES), jnp.float32)

    def run(north_near):
        copies = [
            pltpu.make_async_copy(tails.at[i], out.at[:, pl.ds(CHUNKS[1] * PACK, TAIL)], sem.at[i])
            for i, out in enumerate((near, far) if north_near else (far, near))
        ]
        for copy in copies:
            copy.start()
        for copy in copies:
            copy.wait()

    by_parity(is_even(bins), run)


def border_kernel(bins, own, near, far, field):
    zero = jnp.zeros((ROWS, LANES), jnp.float32)
    for s in range(SUB):
        field[s, :PAD, :] = zero
        field[s, HEIGHT - PAD :, :] = zero
    for d in range(DIRS + 1):
        row = PAD + d * PITCH - SUB
        field[0, row : row + 2 * SUB, :] = zero
    for d in range(DIRS):
        row = PAD + d * PITCH + SUB
        field[0, row : row + ROWS, :] = own[d * ROWS : (d + 1) * ROWS, :]
    tail = CHUNKS[1] * PACK
    halves = [
        jnp.concatenate([ref[0, tail : tail + TAIL, :], ref[1, tail : tail + TAIL, :]], axis=0)
        for ref in (near, far)
    ]
    even = is_even(bins)
    halves = [jnp.where(even, halves[1], halves[0]), jnp.where(even, halves[0], halves[1])]
    for value, is_up in zip(halves, (True, False)):
        for k, d0, count, row in segments(is_up):
            place = PAD + d0 * PITCH + (SUB - k if is_up else SUB + ROWS + k - 1)
            field[0, pl.ds(place, count, stride=PITCH), :] = value[row : row + count]
    speed = jnp.zeros((ROWS, LANES), jnp.float32)
    for f in range(F):
        speed = jnp.where(lane_iota() >= f * STRIP, float(SPEED[f]), speed)
    coefficients = []
    for half in range(2):
        geo = []
        for g in range(3):
            mine = own[(DIRS + g) * ROWS + half * SUB : (DIRS + g) * ROWS + (half + 1) * SUB, :]
            halo = halves[half][PACK + g * SUB : PACK + (g + 1) * SUB]
            geo.append(speed * jnp.concatenate([mine, halo] if half else [halo, mine], axis=0))
        coefficients.append((geo[0], 0.5 * geo[1], 0.5 * geo[2]))
    for step in range(SUB - 1):
        for half in range(2):
            depth, sx, sy = coefficients[half]

            def load(d, shift=0):
                row = PAD + (d % DIRS) * PITCH + half * ROWS + shift
                return field[step, row : row + ROWS, :]

            for d in range(DIRS):
                west, south = COS[d] >= 0.0, SIN[d] >= 0.0
                cos, sin = abs(COS[d]), abs(SIN[d])
                now = load(d)
                up_x = pltpu.roll(now, 1 if west else LANES - 1, 1)
                up_y = load(d, -1 if south else 1)
                vt = SIN[d] * sx - COS[d] * sy
                up_t = jnp.where(vt > 0.0, load(d - 1), load(d + 1))
                moved = depth * (cos * up_x + sin * up_y - (cos + sin) * now) + jnp.abs(vt) * (up_t - now)
                row = PAD + d * PITCH + half * ROWS
                field[step + 1, row : row + ROWS, :] = now + moved


def tables_kernel(bins, near, far, geo_own, depth, turn):
    even = is_even(bins)
    tail = CHUNKS[0] * PACK
    for t in range(TILES):
        whole = []
        for g in range(3):
            rows = slice(tail + g * SUB, tail + (g + 1) * SUB)
            south = jnp.where(even, far[t, rows, :], near[t, rows, :])
            north = jnp.where(even, near[t, rows, :], far[t, rows, :])
            own = geo_own[g, t]
            whole.append([jnp.concatenate([south, own[:SUB]], axis=0), jnp.concatenate([own[SUB:], north], axis=0)])
        for half in range(2):
            depth[t, half * ROWS : (half + 1) * ROWS, :] = whole[0][half]
            sx, sy = 0.5 * whole[1][half], 0.5 * whole[2][half]
            for d in range(DIRS):
                turn[t, d * PITCH + half * ROWS : d * PITCH + (half + 1) * ROWS, :] = SIN[d] * sx - COS[d] * sy


def step_kernel(bins, first, start, count, source_at, *refs):
    even = is_even(bins)
    if first:
        src, near, far, border, geo, turn, out, field_a, field_b, done, sem = refs
    else:
        src, near, far, border, geo, turn, _, out, field_a, field_b, done, sem = refs
    zero = jnp.zeros((ROWS, LANES), jnp.float32)
    for t in range(TILES):
        for field in (field_a, field_b):
            field[t, :PAD, :] = zero
            field[t, HEIGHT - PAD :, :] = zero
        for d in range(DIRS + 1):
            row = PAD + d * PITCH - SUB
            field_a[t, row : row + 2 * SUB, :] = zero
    lanes = lane_iota()
    at_first, at_last = lanes == 0, lanes == LANES - 1
    quarter = DIRS // 4

    def put(i, q):
        slot = lax.rem(i, 2)
        return pltpu.make_async_copy(
            done.at[slot, pl.ds(q * quarter, quarter)],
            out.at[pl.ds((start + i) * DIRS + q * quarter, quarter)],
            sem.at[slot, q],
        )

    def frequency(i, carry):
        base = pl.multiple_of((source_at + i) * SPAN, SPAN)
        for d in range(DIRS):
            row = PAD + d * PITCH + SUB
            for t in range(TILES):
                field_a[t, row : row + ROWS, :] = src[t, pl.ds(base + d * ROWS, ROWS), :]
        def unpack(north_near):
            for ref, is_up in ((near, not north_near), (far, north_near)):
                for k, d0, number, row in segments(is_up):
                    place = PAD + d0 * PITCH + (SUB - k if is_up else SUB + ROWS + k - 1)
                    place = pl.ds(place, number, stride=PITCH)
                    for t in range(TILES):
                        field_a[t, place, :] = ref[t, pl.ds(i * PACK + row, number), :]

        by_parity(even, unpack)

        freq = start + i
        speed = of_freq(SPEED, freq)
        to_first = LANES - (freq * STRIP + SUB - 1)
        to_last = LANES - 1 - (freq * STRIP + SUB + 2)

        @pl.when(i >= 2)
        def _():
            for q in range(4):
                put(i - 2, q).wait()

        def advance(step, old, new):
            last = step == SUB - 1
            for part in (SUB,) if last else (0, ROWS):
                depth = [speed * geo[t, part : part + ROWS, :] for t in range(TILES)]

                def load(d, shift=0):
                    row = PAD + (d % DIRS) * PITCH + part + shift
                    return [old[t, row : row + ROWS, :] for t in range(TILES)]

                before, now = load(-1), load(0)
                initial = now
                for d in range(DIRS):
                    after = load(d + 1) if d < DIRS - 1 else initial
                    west, south = COS[d] >= 0.0, SIN[d] >= 0.0
                    cos, sin = abs(COS[d]), abs(SIN[d])
                    row = PAD + d * PITCH + part
                    outer = pltpu.roll(border[step, row : row + ROWS, :], to_first if west else to_last, 1)
                    rolled = [pltpu.roll(x, 1 if west else LANES - 1, 1) for x in now]
                    up_y = load(d, -1 if south else 1)
                    for t in range(TILES):
                        if west:
                            up_x = jnp.where(at_first, rolled[t - 1] if t else outer, rolled[t])
                        else:
                            up_x = jnp.where(at_last, rolled[t + 1] if t < TILES - 1 else outer, rolled[t])
                        vt = turn[t, d * PITCH + part : d * PITCH + part + ROWS, :]
                        up_t = jnp.where(vt > 0.0, before[t], after[t])
                        if sin == 0.0:
                            moved = depth[t] * (up_x - now[t])
                        elif cos == 0.0:
                            moved = depth[t] * (up_y[t] - now[t])
                        else:
                            moved = depth[t] * (cos * up_x + sin * up_y[t] - (cos + sin) * now[t])
                        value = now[t] + (moved + speed * jnp.abs(vt) * (up_t - now[t]))
                        if last:
                            done[lax.rem(i, 2), d, :, t * LANES : (t + 1) * LANES] = value
                        else:
                            new[t, row : row + ROWS, :] = value
                    before, now = now, after
                    if last and d % quarter == quarter - 1:
                        put(i, d // quarter).start()

        fields = (field_a, field_b)
        for step in range(SUB):
            advance(step, fields[step % 2], fields[(step + 1) % 2])
        return carry

    lax.fori_loop(0, count, frequency, 0)
    for i in range(max(count - 2, 0), count):
        for q in range(4):
            put(i, q).wait()


def after(value, *others):
    return lax.optimization_barrier((value, *others))[0]


def per_device(spectrum, wind_u, wind_v, sea_mask, depth_factor, slope_x, slope_y):
    nbins, rows, cols = spectrum.shape
    assert (nbins, rows, cols) == (F * DIRS, ROWS, TILES * LANES)
    assert lax.axis_size("pt") == 2
    f32 = jnp.float32
    shape = lambda *s: jax.ShapeDtypeStruct(s, f32)
    scratch = lambda *s: pltpu.VMEM(s, f32)
    heights = [c * PACK + (GEO, TAIL, 0, 0)[min(i, 2)] for i, c in enumerate(CHUNKS)]
    params = pltpu.CompilerParams(vmem_limit_bytes=32 * 2**20)
    cost = pl.CostEstimate(flops=1000, bytes_accessed=1000, transcendentals=0)
    tile = (rows, LANES)

    pinned = [
        pltpu.with_memory_space_constraint(x, pltpu.HBM)
        for x in (spectrum, wind_u, wind_v, sea_mask, depth_factor, slope_x, slope_y)
    ]
    bins = lax.axis_size("bin")
    raw, src0, push, damp, geo_own, near0, far0 = pl.pallas_call(
        functools.partial(head_kernel, bins),
        out_shape=[
            shape(TILES, nbins, *tile),
            shape(TILES, CHUNKS[0] * SPAN, LANES),
            shape(TILES, DIRS, *tile),
            shape(TILES, *tile),
            shape(4, TILES, *tile),
            shape(TILES, heights[0], LANES),
            shape(TILES, heights[0], LANES),
        ],
        in_specs=[HBM] * 7,
        out_specs=[VMEM] * 7,
        scratch_shapes=[pltpu.VMEM((rows, cols), x.dtype) for x in (wind_u, wind_v, sea_mask, depth_factor, slope_x, slope_y)]
        + [pltpu.SemaphoreType.DMA((6,)), pltpu.SemaphoreType.DMA((F, TILES))],
        compiler_params=params,
        cost_estimate=cost,
        name="head",
    )(*pinned)

    n = len(CHUNKS) - 1
    outs = pl.pallas_call(
        functools.partial(rest_kernel, bins),
        out_shape=[
            shape(TILES, (F - CHUNKS[0]) * SPAN, LANES),
            shape(EDGES * rows, LANES),
            *[shape(TILES, h, LANES) for h in heights[1:]] * 2,
        ],
        in_specs=[VMEM] * 5,
        out_specs=[VMEM] * (2 + 2 * n),
        compiler_params=params,
        cost_estimate=cost,
        name="rest",
    )(raw, src0, push, damp, geo_own)
    src, edge = outs[:2]
    nears, fars = [near0, *outs[2 : 2 + n]], [far0, *outs[2 + n :]]

    blocks = lax.axis_size("region") * bins

    def exchange(value, odd):
        pairs = [(i, i + 1) for i in range(odd, blocks - 1, 2)]
        return lax.ppermute(value, ("region", "bin"), pairs + [(j, i) for i, j in pairs])

    from_near, from_far = [exchange(nears[0], 0)], [exchange(fars[0], 1)]
    depth, turn = pl.pallas_call(
        functools.partial(tables_kernel, bins),
        out_shape=[shape(TILES, PITCH, LANES), shape(TILES, DIRS * PITCH, LANES)],
        in_specs=[VMEM] * 3,
        out_specs=[VMEM] * 2,
        compiler_params=params,
        cost_estimate=pl.CostEstimate(flops=100_000_000_000, bytes_accessed=1000, transcendentals=0),
        name="tables",
    )(from_near[0], from_far[0], geo_own)
    other = lax.ppermute(edge, "pt", [(0, 1), (1, 0)])
    edge, nears[1], fars[1] = pl.pallas_call(
        functools.partial(join_kernel, bins),
        out_shape=[shape(EDGES * rows, LANES), shape(TILES, heights[1], LANES), shape(TILES, heights[1], LANES)],
        in_specs=[VMEM, VMEM, ANY, ANY],
        out_specs=[VMEM, ANY, ANY],
        scratch_shapes=[scratch(2, TILES, TAIL, LANES), pltpu.SemaphoreType.DMA((2,))],
        input_output_aliases={2: 1, 3: 2},
        compiler_params=params,
        cost_estimate=cost,
        name="join",
    )(edge, other, nears[1], fars[1])
    from_near += [exchange(nears[1], 0), exchange(after(nears[2], depth), 0)]
    from_far.append(exchange(fars[1], 1))
    border = pl.pallas_call(
        functools.partial(border_kernel, bins),
        out_shape=shape(SUB, HEIGHT, LANES),
        in_specs=[VMEM] * 3,
        out_specs=VMEM,
        compiler_params=params,
        cost_estimate=cost,
        name="border",
    )(edge, from_near[1], from_far[1])


    from_far.append(exchange(after(fars[2], border), 1))

    start, result = 0, None
    for c, count in enumerate(CHUNKS):
        first = c == 0
        operands = [src0 if first else src, from_near[c], from_far[c], border, depth, turn]
        in_specs = [VMEM] * 6
        out_shape = [shape(nbins, rows, cols)]
        aliases = {}
        if not first:
            operands.append(result)
            in_specs.append(ANY)
            aliases = {len(operands) - 1: 0}

        def kernel(*refs, first=first, start=start, count=count):
            step_kernel(bins, first, start, count, start - (0 if first else CHUNKS[0]), *refs)

        outs = pl.pallas_call(
            kernel,
            out_shape=out_shape,
            in_specs=in_specs,
            out_specs=[ANY, VMEM][: len(out_shape)],
            scratch_shapes=[scratch(TILES, HEIGHT, LANES)] * 2
            + [scratch(2, DIRS, rows, cols), pltpu.SemaphoreType.DMA((2, 4))],
            input_output_aliases=aliases,
            compiler_params=params,
            cost_estimate=cost,
            name=f"steps_{c}",
        )(*operands)
        result = outs[0]
        if first:
            for later in range(3, len(CHUNKS)):
                value, other, result = lax.optimization_barrier((nears[later], fars[later], result))
                from_near.append(exchange(value, 0))
                from_far.append(exchange(other, 1))
        start += count
    return result


def solution(mesh):
    in_specs = (
        P("ens", ("region", "bin"), "pt"),
        P(("ens", "region", "bin"), "pt"),
        P(("ens", "region", "bin"), "pt"),
        P("region", "pt"),
        P("region", "pt"),
        P("region", "pt"),
        P("region", "pt"),
    )
    out_specs = P("ens", ("region", "bin"), "pt")
    return jax.shard_map(
        per_device, mesh=mesh, in_specs=in_specs, out_specs=out_specs, check_vma=False
    )
```

```python
import functools
import math

import jax
import jax.numpy as jnp
import numpy as np
from jax import lax
from jax.experimental import pallas as pl
from jax.experimental.pallas import tpu as pltpu
from jax.sharding import PartitionSpec as P

F = 12
DIRS = 36
SUB = 4
ROWS = 8
LANES = 128
TILES = 2
HALF = DIRS // 2
SENT = [HALF - 1 + 2 * (SUB - k) for k in range(1, SUB + 1)]
PACK = sum(SENT)
GEO = 16
CHUNKS = (3, 2, 4, 3)
STRIP = 2 * SUB + 2
EDGES = DIRS + 3
TAIL = 48
PITCH = ROWS + 2 * SUB
PAD = 8
HEIGHT = DIRS * PITCH + 2 * PAD
SPAN = DIRS * ROWS

SIGMA = 0.6 * 1.1 ** np.arange(F, dtype=np.float64)
WEIGHT = SIGMA / (DIRS * SIGMA.sum())


def quarter_exact(fn):
    values = np.array([fn(2.0 * math.pi * d / DIRS) for d in range(DIRS)])
    values[np.abs(values) < 1e-9] = 0.0
    return [float(x) for x in values]


COS = quarter_exact(math.cos)
SIN = quarter_exact(math.sin)
SPEED = 0.27 / SIGMA


def of_freq(values, f):
    if isinstance(f, int):
        return float(values[f])
    out = jnp.float32(values[0])
    for i in range(1, F):
        out = jnp.where(f == i, jnp.float32(values[i]), out)
    return out


HBM = pl.BlockSpec(memory_space=pltpu.HBM)
VMEM = pl.BlockSpec(memory_space=pltpu.VMEM)
ANY = pl.BlockSpec(memory_space=pl.ANY)


def segments(up):
    out, row = [], 0
    for k in range(1, SUB + 1):
        low = 1 - (SUB - k) + (0 if up else HALF)
        left, at = SENT[k - 1], low
        while left > 0:
            first = at % DIRS
            count = min(left, DIRS - first)
            out.append((k, first, count, row))
            row, at, left = row + count, at + count, left - count
    return out


def lane_iota():
    return lax.broadcasted_iota(jnp.int32, (ROWS, LANES), 1)


def own_lanes():
    own = jnp.zeros((ROWS, LANES), jnp.bool_)
    for f in range(F):
        own = own | (lane_iota() == f * STRIP + SUB) | (lane_iota() == f * STRIP + SUB + 1)
    return own


def put_edges(pairs):
    lanes = lane_iota()
    packed = jnp.zeros((ROWS, LANES), jnp.float32)
    for f, (first_tile, last_tile) in enumerate(pairs):
        ends = jnp.where(lanes < LANES // 2, first_tile, last_tile)
        at = f * STRIP
        packed = jnp.where(lanes >= at, pltpu.roll(ends, (at + SUB) % LANES, 1), packed)
        packed = jnp.where(lanes >= at + SUB + 1, pltpu.roll(ends, (at + SUB + 2) % LANES, 1), packed)
    return packed


def is_even(bins):
    return lax.rem(lax.axis_index("region") * bins + lax.axis_index("bin"), 2) == 0


def by_parity(even, run):
    pl.when(even)(lambda: run(True))
    pl.when(jnp.logical_not(even))(lambda: run(False))


def split(value):
    return value[:, :LANES], value[:, LANES:]


def make_sources(raw, src, push, inverse, f, base):
    sig = of_freq(SIGMA, f)
    for t in range(TILES):
        for d in range(DIRS):
            grown = raw[t, f * DIRS + d] * (1.0 + sig * push[t, d])
            row = base + d * ROWS
            src[t, pl.ds(row, ROWS), :] = grown * inverse[t]


def make_packs(even, src, base, local, near, far):
    def run(north_near):
        for ref, up in ((near, north_near), (far, not north_near)):
            for k, d0, count, row in segments(up):
                j = ROWS - k if up else k - 1
                for t in range(TILES):
                    value = src[t, pl.ds(base + d0 * ROWS + j, count, stride=ROWS), :]
                    ref[t, pl.ds(local * PACK + row, count), :] = value

    by_parity(even, run)


def head_kernel(
    bins, spec, u_hbm, v_hbm, mask_hbm, depth_hbm, sx_hbm, sy_hbm,
    raw, src0, push, damp_ref, geo, near, far,
    u_ref, v_ref, mask_ref, depth_ref, sx_ref, sy_ref, small_sem, in_sem,
):
    even = is_even(bins)
    off = pl.multiple_of(lax.axis_index("bin") * ROWS, ROWS)
    own = pl.ds(off, ROWS)
    small = [
        pltpu.make_async_copy(a, b, small_sem.at[i])
        for i, (a, b) in enumerate(
            (
                (u_hbm, u_ref),
                (v_hbm, v_ref),
                (mask_hbm.at[own], mask_ref),
                (depth_hbm.at[own], depth_ref),
                (sx_hbm.at[own], sx_ref),
                (sy_hbm.at[own], sy_ref),
            )
        )
    ]

    def load(f, t):
        return pltpu.make_async_copy(
            spec.at[pl.ds(f * DIRS, DIRS), :, pl.ds(t * LANES, LANES)],
            raw.at[t, pl.ds(f * DIRS, DIRS)],
            in_sem.at[f, t],
        )

    for copy in small:
        copy.start()
    for f in range(F):
        for t in range(TILES):
            load(f, t).start()
    for copy in small:
        copy.wait()

    mask = mask_ref[...].astype(jnp.float32)
    fields = (depth_ref[...] * mask, sx_ref[...] * mask, sy_ref[...] * mask)
    tail = CHUNKS[0] * PACK
    for g in range(3):
        for t, tile in enumerate(split(fields[g])):
            geo[g, t] = tile
        rows = slice(tail + g * SUB, tail + (g + 1) * SUB)
        for t, tile in enumerate(split(fields[g])):
            near[t, rows, :] = jnp.where(even, tile[ROWS - SUB :, :], tile[:SUB, :])
            far[t, rows, :] = jnp.where(even, tile[:SUB, :], tile[ROWS - SUB :, :])
    for ref in (near, far):
        for t in range(TILES):
            ref[t, tail + 3 * SUB :, :] = jnp.zeros((GEO - 3 * SUB, LANES), jnp.float32)
    for t, tile in enumerate(split(mask)):
        geo[3, t] = tile
    u, v = split(u_ref[...]), split(v_ref[...])
    for d in range(DIRS):
        for t in range(TILES):
            lean = jnp.maximum(u[t] * COS[d] + v[t] * SIN[d], 0.0)
            push[t, d] = 0.5 * lean * lean

    zero = jnp.zeros((ROWS, LANES), jnp.float32)
    sums = [(zero, zero)] * TILES
    for f in range(F):
        for t in range(TILES):
            load(f, t).wait()
            parts = [raw[t, f * DIRS + d] for d in range(4)]
            for d in range(4, DIRS):
                parts[d % 4] = parts[d % 4] + raw[t, f * DIRS + d]
            total = (parts[0] + parts[1]) + (parts[2] + parts[3])
            energy, first = sums[t]
            sums[t] = energy + float(WEIGHT[f]) * total, first + float(WEIGHT[f] * SIGMA[f]) * total
    damps = []
    for t, (energy, first) in enumerate(sums):
        mean_sigma = first / energy
        steep = energy * mean_sigma * mean_sigma / 1.5
        damps.append(0.5 * steep * steep / mean_sigma)
        damp_ref[t] = damps[t]

    def body(f, carry):
        inverse = [geo[3, t] / (1.0 + of_freq(SIGMA, f) * damps[t]) for t in range(TILES)]
        base = pl.multiple_of(f * SPAN, SPAN)
        make_sources(raw, src0, push, inverse, f, base)
        make_packs(even, src0, base, f, near, far)
        return carry

    lax.fori_loop(0, CHUNKS[0], body, 0)


def rest_kernel(bins, raw, src0, push, damp, geo, *refs):
    n = len(CHUNKS) - 1
    src, edge = refs[:2]
    nears, fars = refs[2 : 2 + n], refs[2 + n :]
    even = is_even(bins)
    at = CHUNKS[0]
    for c in range(n):
        def body(local, carry, c=c, at=at):
            f = at + local
            inverse = [geo[3, t] / (1.0 + of_freq(SIGMA, f) * damp[t]) for t in range(TILES)]
            base = pl.multiple_of((f - CHUNKS[0]) * SPAN, SPAN)
            make_sources(raw, src, push, inverse, f, base)
            make_packs(even, src, base, local, nears[c], fars[c])
            return carry

        lax.fori_loop(0, CHUNKS[c + 1], body, 0)
        at += CHUNKS[c + 1]

    def edges(d, carry):
        pairs = []
        for f in range(F):
            ref, local = (src0, f) if f < CHUNKS[0] else (src, f - CHUNKS[0])
            row = pl.ds(pl.multiple_of(local * SPAN + d * ROWS, ROWS), ROWS)
            pairs.append((ref[0, row, :], ref[1, row, :]))
        edge[pl.ds(pl.multiple_of(d * ROWS, ROWS), ROWS), :] = put_edges(pairs)
        return carry

    lax.fori_loop(0, DIRS, edges, 0, unroll=4)
    for g in range(3):
        edge[(DIRS + g) * ROWS : (DIRS + g + 1) * ROWS, :] = put_edges([(geo[g, 0], geo[g, 1])] * F)


def join_kernel(bins, own, other, near_in, far_in, edge, near, far, tails, sem):
    lanes = own_lanes()
    for d in range(EDGES):
        rows = slice(d * ROWS, (d + 1) * ROWS)
        edge[rows, :] = jnp.where(lanes, own[rows, :], other[rows, :])
    for i, up in enumerate((True, False)):
        pieces = [
            (row, count, pl.ds(d0 * ROWS + (ROWS - k if up else k - 1), count, stride=ROWS))
            for k, d0, count, row in segments(up)
        ]
        for g in range(3):
            pieces.append((PACK + g * SUB, SUB, pl.ds((DIRS + g) * ROWS + (ROWS - SUB if up else 0), SUB)))
        for row, count, place in pieces:
            value, at = edge[place, :], 0
            while at < count:
                half, inner = divmod(row + at, TAIL)
                size = min(count - at, TAIL - inner)
                tails[i, half, inner : inner + size, :] = value[at : at + size]
                at += size
        rest = 2 * TAIL - PACK - 3 * SUB
        tails[i, 1, TAIL - rest :, :] = jnp.zeros((rest, LANES), jnp.float32)

    def run(north_near):
        copies = [
            pltpu.make_async_copy(tails.at[i], out.at[:, pl.ds(CHUNKS[1] * PACK, TAIL)], sem.at[i])
            for i, out in enumerate((near, far) if north_near else (far, near))
        ]
        for copy in copies:
            copy.start()
        for copy in copies:
            copy.wait()

    by_parity(is_even(bins), run)


def border_kernel(bins, own, near, far, field):
    zero = jnp.zeros((ROWS, LANES), jnp.float32)
    for s in range(SUB):
        field[s, :PAD, :] = zero
        field[s, HEIGHT - PAD :, :] = zero
    for d in range(DIRS + 1):
        row = PAD + d * PITCH - SUB
        field[0, row : row + 2 * SUB, :] = zero
    for d in range(DIRS):
        row = PAD + d * PITCH + SUB
        field[0, row : row + ROWS, :] = own[d * ROWS : (d + 1) * ROWS, :]
    tail = CHUNKS[1] * PACK
    halves = [
        jnp.concatenate([ref[0, tail : tail + TAIL, :], ref[1, tail : tail + TAIL, :]], axis=0)
        for ref in (near, far)
    ]
    even = is_even(bins)
    halves = [jnp.where(even, halves[1], halves[0]), jnp.where(even, halves[0], halves[1])]
    for value, is_up in zip(halves, (True, False)):
        for k, d0, count, row in segments(is_up):
            place = PAD + d0 * PITCH + (SUB - k if is_up else SUB + ROWS + k - 1)
            field[0, pl.ds(place, count, stride=PITCH), :] = value[row : row + count]
    speed = jnp.zeros((ROWS, LANES), jnp.float32)
    for f in range(F):
        speed = jnp.where(lane_iota() >= f * STRIP, float(SPEED[f]), speed)
    coefficients = []
    for half in range(2):
        geo = []
        for g in range(3):
            mine = own[(DIRS + g) * ROWS + half * SUB : (DIRS + g) * ROWS + (half + 1) * SUB, :]
            halo = halves[half][PACK + g * SUB : PACK + (g + 1) * SUB]
            geo.append(speed * jnp.concatenate([mine, halo] if half else [halo, mine], axis=0))
        coefficients.append((geo[0], 0.5 * geo[1], 0.5 * geo[2]))
    for step in range(SUB - 1):
        for half in range(2):
            depth, sx, sy = coefficients[half]

            def load(d, shift=0):
                row = PAD + (d % DIRS) * PITCH + half * ROWS + shift
                return field[step, row : row + ROWS, :]

            for d in range(DIRS):
                west, south = COS[d] >= 0.0, SIN[d] >= 0.0
                cos, sin = abs(COS[d]), abs(SIN[d])
                now = load(d)
                up_x = pltpu.roll(now, 1 if west else LANES - 1, 1)
                up_y = load(d, -1 if south else 1)
                vt = SIN[d] * sx - COS[d] * sy
                up_t = jnp.where(vt > 0.0, load(d - 1), load(d + 1))
                moved = depth * (cos * up_x + sin * up_y - (cos + sin) * now) + jnp.abs(vt) * (up_t - now)
                row = PAD + d * PITCH + half * ROWS
                field[step + 1, row : row + ROWS, :] = now + moved


def tables_kernel(bins, near, far, geo_own, depth, turn):
    even = is_even(bins)
    tail = CHUNKS[0] * PACK
    for t in range(TILES):
        whole = []
        for g in range(3):
            rows = slice(tail + g * SUB, tail + (g + 1) * SUB)
            south = jnp.where(even, far[t, rows, :], near[t, rows, :])
            north = jnp.where(even, near[t, rows, :], far[t, rows, :])
            own = geo_own[g, t]
            whole.append([jnp.concatenate([south, own[:SUB]], axis=0), jnp.concatenate([own[SUB:], north], axis=0)])
        for half in range(2):
            depth[t, half * ROWS : (half + 1) * ROWS, :] = whole[0][half]
            sx, sy = 0.5 * whole[1][half], 0.5 * whole[2][half]
            for d in range(DIRS):
                turn[t, d * PITCH + half * ROWS : d * PITCH + (half + 1) * ROWS, :] = SIN[d] * sx - COS[d] * sy


def step_kernel(bins, first, start, count, source_at, *refs):
    even = is_even(bins)
    if first:
        src, near, far, border, geo, turn, out, field_a, field_b, done, sem = refs
    else:
        src, near, far, border, geo, turn, _, out, field_a, field_b, done, sem = refs
    zero = jnp.zeros((ROWS, LANES), jnp.float32)
    for t in range(TILES):
        for field in (field_a, field_b):
            field[t, :PAD, :] = zero
            field[t, HEIGHT - PAD :, :] = zero
        for d in range(DIRS + 1):
            row = PAD + d * PITCH - SUB
            field_a[t, row : row + 2 * SUB, :] = zero
    lanes = lane_iota()
    at_first, at_last = lanes == 0, lanes == LANES - 1
    quarter = DIRS // 4

    def put(i, q):
        slot = lax.rem(i, 2)
        return pltpu.make_async_copy(
            done.at[slot, pl.ds(q * quarter, quarter)],
            out.at[pl.ds((start + i) * DIRS + q * quarter, quarter)],
            sem.at[slot, q],
        )

    def frequency(i, carry):
        base = pl.multiple_of((source_at + i) * SPAN, SPAN)
        for d in range(DIRS):
            row = PAD + d * PITCH + SUB
            for t in range(TILES):
                field_a[t, row : row + ROWS, :] = src[t, pl.ds(base + d * ROWS, ROWS), :]
        def unpack(north_near):
            for ref, is_up in ((near, not north_near), (far, north_near)):
                for k, d0, number, row in segments(is_up):
                    place = PAD + d0 * PITCH + (SUB - k if is_up else SUB + ROWS + k - 1)
                    place = pl.ds(place, number, stride=PITCH)
                    for t in range(TILES):
                        field_a[t, place, :] = ref[t, pl.ds(i * PACK + row, number), :]

        by_parity(even, unpack)

        freq = start + i
        speed = of_freq(SPEED, freq)
        to_first = LANES - (freq * STRIP + SUB - 1)
        to_last = LANES - 1 - (freq * STRIP + SUB + 2)

        @pl.when(i >= 2)
        def _():
            for q in range(4):
                put(i - 2, q).wait()

        def advance(step, old, new):
            last = step == SUB - 1
            for part in (SUB,) if last else (0, ROWS):
                depth = [speed * geo[t, part : part + ROWS, :] for t in range(TILES)]

                def load(d, shift=0):
                    row = PAD + (d % DIRS) * PITCH + part + shift
                    return [old[t, row : row + ROWS, :] for t in range(TILES)]

                before, now = load(-1), load(0)
                initial = now
                for d in range(DIRS):
                    after = load(d + 1) if d < DIRS - 1 else initial
                    west, south = COS[d] >= 0.0, SIN[d] >= 0.0
                    cos, sin = abs(COS[d]), abs(SIN[d])
                    row = PAD + d * PITCH + part
                    outer = pltpu.roll(border[step, row : row + ROWS, :], to_first if west else to_last, 1)
                    rolled = [pltpu.roll(x, 1 if west else LANES - 1, 1) for x in now]
                    up_y = load(d, -1 if south else 1)
                    for t in range(TILES):
                        if west:
                            up_x = jnp.where(at_first, rolled[t - 1] if t else outer, rolled[t])
                        else:
                            up_x = jnp.where(at_last, rolled[t + 1] if t < TILES - 1 else outer, rolled[t])
                        vt = turn[t, d * PITCH + part : d * PITCH + part + ROWS, :]
                        up_t = jnp.where(vt > 0.0, before[t], after[t])
                        if sin == 0.0:
                            moved = depth[t] * (up_x - now[t])
                        elif cos == 0.0:
                            moved = depth[t] * (up_y[t] - now[t])
                        else:
                            moved = depth[t] * (cos * up_x + sin * up_y[t] - (cos + sin) * now[t])
                        value = now[t] + (moved + speed * jnp.abs(vt) * (up_t - now[t]))
                        if last:
                            done[lax.rem(i, 2), d, :, t * LANES : (t + 1) * LANES] = value
                        else:
                            new[t, row : row + ROWS, :] = value
                    before, now = now, after
                    if last and d % quarter == quarter - 1:
                        put(i, d // quarter).start()

        fields = (field_a, field_b)
        for step in range(SUB):
            advance(step, fields[step % 2], fields[(step + 1) % 2])
        return carry

    lax.fori_loop(0, count, frequency, 0)
    for i in range(max(count - 2, 0), count):
        for q in range(4):
            put(i, q).wait()


def after(value, *others):
    return lax.optimization_barrier((value, *others))[0]


def per_device(spectrum, wind_u, wind_v, sea_mask, depth_factor, slope_x, slope_y):
    nbins, rows, cols = spectrum.shape
    assert (nbins, rows, cols) == (F * DIRS, ROWS, TILES * LANES)
    assert lax.axis_size("pt") == 2
    f32 = jnp.float32
    shape = lambda *s: jax.ShapeDtypeStruct(s, f32)
    scratch = lambda *s: pltpu.VMEM(s, f32)
    heights = [c * PACK + (GEO, TAIL, 0, 0)[min(i, 2)] for i, c in enumerate(CHUNKS)]
    params = pltpu.CompilerParams(vmem_limit_bytes=32 * 2**20)
    cost = pl.CostEstimate(flops=1000, bytes_accessed=1000, transcendentals=0)
    tile = (rows, LANES)

    pinned = [
        pltpu.with_memory_space_constraint(x, pltpu.HBM)
        for x in (spectrum, wind_u, wind_v, sea_mask, depth_factor, slope_x, slope_y)
    ]
    bins = lax.axis_size("bin")
    raw, src0, push, damp, geo_own, near0, far0 = pl.pallas_call(
        functools.partial(head_kernel, bins),
        out_shape=[
            shape(TILES, nbins, *tile),
            shape(TILES, CHUNKS[0] * SPAN, LANES),
            shape(TILES, DIRS, *tile),
            shape(TILES, *tile),
            shape(4, TILES, *tile),
            shape(TILES, heights[0], LANES),
            shape(TILES, heights[0], LANES),
        ],
        in_specs=[HBM] * 7,
        out_specs=[VMEM] * 7,
        scratch_shapes=[pltpu.VMEM((rows, cols), x.dtype) for x in (wind_u, wind_v, sea_mask, depth_factor, slope_x, slope_y)]
        + [pltpu.SemaphoreType.DMA((6,)), pltpu.SemaphoreType.DMA((F, TILES))],
        compiler_params=params,
        cost_estimate=cost,
        name="head",
    )(*pinned)

    n = len(CHUNKS) - 1
    outs = pl.pallas_call(
        functools.partial(rest_kernel, bins),
        out_shape=[
            shape(TILES, (F - CHUNKS[0]) * SPAN, LANES),
            shape(EDGES * rows, LANES),
            *[shape(TILES, h, LANES) for h in heights[1:]] * 2,
        ],
        in_specs=[VMEM] * 5,
        out_specs=[VMEM] * (2 + 2 * n),
        compiler_params=params,
        cost_estimate=cost,
        name="rest",
    )(raw, src0, push, damp, geo_own)
    src, edge = outs[:2]
    nears, fars = [near0, *outs[2 : 2 + n]], [far0, *outs[2 + n :]]

    blocks = lax.axis_size("region") * bins

    def exchange(value, odd):
        pairs = [(i, i + 1) for i in range(odd, blocks - 1, 2)]
        return lax.ppermute(value, ("region", "bin"), pairs + [(j, i) for i, j in pairs])

    from_near, from_far = [exchange(nears[0], 0)], [exchange(fars[0], 1)]
    depth, turn = pl.pallas_call(
        functools.partial(tables_kernel, bins),
        out_shape=[shape(TILES, PITCH, LANES), shape(TILES, DIRS * PITCH, LANES)],
        in_specs=[VMEM] * 3,
        out_specs=[VMEM] * 2,
        compiler_params=params,
        cost_estimate=pl.CostEstimate(flops=100_000_000_000, bytes_accessed=1000, transcendentals=0),
        name="tables",
    )(from_near[0], from_far[0], geo_own)
    other = lax.ppermute(edge, "pt", [(0, 1), (1, 0)])
    edge, nears[1], fars[1] = pl.pallas_call(
        functools.partial(join_kernel, bins),
        out_shape=[shape(EDGES * rows, LANES), shape(TILES, heights[1], LANES), shape(TILES, heights[1], LANES)],
        in_specs=[VMEM, VMEM, ANY, ANY],
        out_specs=[VMEM, ANY, ANY],
        scratch_shapes=[scratch(2, TILES, TAIL, LANES), pltpu.SemaphoreType.DMA((2,))],
        input_output_aliases={2: 1, 3: 2},
        compiler_params=params,
        cost_estimate=cost,
        name="join",
    )(edge, other, nears[1], fars[1])
    from_near += [exchange(nears[1], 0), exchange(after(nears[2], depth), 0)]
    from_far.append(exchange(fars[1], 1))
    border = pl.pallas_call(
        functools.partial(border_kernel, bins),
        out_shape=shape(SUB, HEIGHT, LANES),
        in_specs=[VMEM] * 3,
        out_specs=VMEM,
        compiler_params=params,
        cost_estimate=cost,
        name="border",
    )(edge, from_near[1], from_far[1])


    from_far.append(exchange(after(fars[2], depth), 1))

    start, result = 0, None
    for c, count in enumerate(CHUNKS):
        first = c == 0
        operands = [src0 if first else src, from_near[c], from_far[c], border, depth, turn]
        in_specs = [VMEM] * 6
        out_shape = [shape(nbins, rows, cols)]
        aliases = {}
        if not first:
            operands.append(result)
            in_specs.append(ANY)
            aliases = {len(operands) - 1: 0}

        def kernel(*refs, first=first, start=start, count=count):
            step_kernel(bins, first, start, count, start - (0 if first else CHUNKS[0]), *refs)

        outs = pl.pallas_call(
            kernel,
            out_shape=out_shape,
            in_specs=in_specs,
            out_specs=[ANY, VMEM][: len(out_shape)],
            scratch_shapes=[scratch(TILES, HEIGHT, LANES)] * 2
            + [scratch(2, DIRS, rows, cols), pltpu.SemaphoreType.DMA((2, 4))],
            input_output_aliases=aliases,
            compiler_params=params,
            cost_estimate=cost,
            name=f"steps_{c}",
        )(*operands)
        result = outs[0]
        if first:
            for later in range(3, len(CHUNKS)):
                value, other, result = lax.optimization_barrier((nears[later], fars[later], result))
                from_near.append(exchange(value, 0))
                from_far.append(exchange(other, 1))
        start += count
    return result


def solution(mesh):
    in_specs = (
        P("ens", ("region", "bin"), "pt"),
        P(("ens", "region", "bin"), "pt"),
        P(("ens", "region", "bin"), "pt"),
        P("region", "pt"),
        P("region", "pt"),
        P("region", "pt"),
        P("region", "pt"),
    )
    out_specs = P("ens", ("region", "bin"), "pt")
    return jax.shard_map(
        per_device, mesh=mesh, in_specs=in_specs, out_specs=out_specs, check_vma=False
    )
```
